256 devices in a mesh: role: 2 (over y_hi), dp: 2 (over y_lo), expert: 64 (over x, z, core).
Axes of the slice: x: 4, y: 4 (y_hi: 2, y_lo: 2; y = y_hi * 2 + y_lo), z: 8, core: 2. Of those that a mesh axis runs over, the one named last changes fastest.
Arguments:
- prompt_pool: bfloat16 [2, 2, 64, 20, 64, 576], P('role', 'dp', 'expert'), may hold values from -6 to 6
- block_table: int32 [2, 2, 64, 4, 4], P(None, 'dp', 'expert'), may hold values from 0 to 19, as said below
- cache_len: int32 [2, 2, 4], P('role', 'dp'), may hold values from 1 to 16384, as said below
- queries: bfloat16 [2, 2, 2, 4, 64, 576], P(None, 'role', 'dp')
- fresh_latent: bfloat16 [2, 2, 2, 4, 576], P(None, 'role', 'dp'), may hold values from -6 to 6
- x_in: bfloat16 [2, 2, 2, 4, 7168], P(None, 'role', 'dp', None, 'expert'), may hold values from -4 to 4
- routes: int32 [2, 2, 2, 4, 8], P(None, 'role', 'dp'), may hold values from 0 to 15, all different within a row; in each aligned block of 4 rows (0 to 3, 4 to 7, ..., all dimensions but the last counted through in order) at most 3 rows name the same one
- gates: float32 [2, 2, 2, 4, 8], P(None, 'role', 'dp'), may hold values from 0.2 to 1
- norm_gain: float32 [7168], replicated, may hold values from 0.5 to 1.5
- value_up: bfloat16 [64, 512, 128], P('expert'), may hold values from -0.25 to 0.25
- out_proj: bfloat16 [8192, 7168], P('expert'), may hold values from -0.1875 to 0.1875
- w_gate: bfloat16 [128, 7168, 128], P(('dp', 'expert')), may hold values from -0.0625 to 0.0625
- w_up: bfloat16 [128, 7168, 128], P(('dp', 'expert')), may hold values from -0.0625 to 0.0625
- w_down: bfloat16 [128, 128, 7168], P(('dp', 'expert')), may hold values from -0.1875 to 0.1875
Outputs:
- layer_out: bfloat16 [2, 2, 2, 4, 7168], P(None, 'role', 'dp', None, 'expert')
The draws below stay inside these ranges and needn't reach their ends.
Inputs may be any that keep to these rules, and one draw needn't show every extreme that they name: `block_table`: within one device's table (fixed r, d, e) the 16 slots differ. `cache_len`: some request of every group has all 16384 positions cached. `routes`: in each step, at most 3 of one group's 4 requests name the same expert; a request's 8 experts differ.
All inputs are finite; a program needn't handle non-finite values.
Results may differ from the reference program's by a relative error of at most 0.014.
Values may be sent and summed in bfloat16 or wider, within the bound.
No kernel may reach another device: no remote copies, remote signals or barrier semaphores. Data moves between devices by JAX's collectives and lax.ppermute only.
A program may use at most 192 MiB of HBM per device.

```python
import math
import jax
import jax.numpy as jnp
import numpy as np
from jax import lax

D = 7168
LAT = 512
KV = 576
VHEAD = 128
HEADS = 64
SLICES = 8
HID_DEV = 128
EXP_WIDTH = 1024
EXPERTS = 16
TOP = 8
REQ = 4
CAP = 3
BLK = 64
NBLK = 4
POOL = 20
STEPS = 2
N_ROLE = 2
N_DP = 2
N_EXPERT = 64


def draw_block_table(key, part):
    key = jax.random.fold_in(key, 23)
    total_count = N_ROLE * N_DP * N_EXPERT
    key_list = jax.random.split(key, total_count)
    orders = jax.vmap(lambda one_key: jax.random.permutation(one_key, POOL))(key_list)
    return orders[:, :REQ * NBLK].reshape(N_ROLE, N_DP, N_EXPERT, REQ, NBLK).astype(jnp.int32)


def draw_cache_len(key, part):
    key = jax.random.fold_in(key, 37)
    length_key, full_key = jax.random.split(key)
    longest = NBLK * BLK * N_EXPERT
    lengths = jax.random.randint(length_key, (N_ROLE, N_DP, REQ), 1, longest + 1)
    chosen = jax.random.randint(full_key, (N_ROLE, N_DP, 1), 0, REQ)
    places = lax.broadcasted_iota(jnp.int32, (N_ROLE, N_DP, REQ), 2)
    return jnp.where(places == chosen, longest, lengths).astype(jnp.int32)


def draw_queries(key, part):
    key = jax.random.fold_in(key, 11)
    base_key = jax.random.fold_in(key, 0)
    values = jax.random.normal(base_key, (STEPS, N_ROLE, N_DP, REQ, HEADS, KV), jnp.float32)
    return values.astype(jnp.bfloat16)


def raised(drawn, own_key, source, target, shards_of, factor):
    def block_of(position):
        return (jnp.arange(drawn.shape[position]) // (drawn.shape[position] // shards_of)).reshape((-1,) + (1,) * (drawn.ndim - 1 - position))

    near = jax.random.permutation(own_key, shards_of)[block_of(target)]
    other_side = (block_of(target) + shards_of // 2) % shards_of
    return jnp.where((block_of(source) == near) | (block_of(source) == other_side), factor * drawn, drawn)


def level_of(stream_key, shape, pieces, low, largest):
    level = 1.0
    for axis_at, parts in pieces:
        draws = jax.random.uniform(jax.random.fold_in(jax.random.fold_in(stream_key, 6), axis_at), (parts,), jnp.float32, low / len(pieces), largest / len(pieces))
        level = level * jnp.repeat(jnp.exp(draws), shape[axis_at] // parts).reshape((-1,) + (1,) * (len(shape) - 1 - axis_at))
    return level


def deal_out(stream_key, own, number, rows, count, top, limit, skew):
    order = jax.random.permutation(stream_key, count)
    crowded, ordinary = shares(count, rows * top, limit, skew, True), shares(count, rows * top, limit, skew, False)
    places = jnp.arange(count)

    def named(tallies, rotation):
        used = int((tallies > 0).sum())
        fixed = max(1, used // 4)
        shifted = fixed + (places - fixed + rotation * (used - fixed)) % max(1, count - fixed)
        return jnp.zeros((count,), jnp.int32).at[order[jnp.where(places < fixed, places, shifted)]].set(jnp.asarray(tallies, jnp.int32))

    tallies = jnp.where(number % 4 == 0, named(crowded, number // 4), named(ordinary, number - number // 4 - 1))
    mixed = jax.random.permutation(jax.random.fold_in(own, 3), count)
    giver, receiver = mixed[0:count // 2 * 2:2], mixed[1:count // 2 * 2:2]
    slack = jnp.minimum(tallies[giver] - 1, limit - tallies[receiver]) // 2
    slack = jnp.where((giver == order[0]) | (receiver == order[0]) | (tallies[receiver] == 0), 0, jnp.maximum(slack, 0))
    shifted = jax.random.randint(jax.random.fold_in(own, 4), (count // 2,), 0, 1 << 20) % (slack + 1)
    tallies = tallies.at[giver].add(-shifted).at[receiver].add(shifted)
    labels = jnp.searchsorted(jnp.cumsum(tallies), jnp.arange(rows * top), side="right").astype(jnp.int32)
    grid = labels.reshape(top, rows).T
    grid = grid[jax.random.permutation(jax.random.fold_in(own, 1), rows)]
    rotation = jax.random.randint(jax.random.fold_in(own, 2), (rows, 1), 0, top)
    return jnp.take_along_axis(grid, (jnp.arange(top)[None, :] + rotation) % top, axis=1)


def shares(count, total, most, slope, full):
    portions = [(1 << 20) // math.isqrt(standing ** slope) + 1 for standing in range(1, count + 1)]
    largest = most if full else min(most, max(-(-total // count), total * portions[0] // sum(portions)))
    least = 1 if total - largest >= count - 1 else 0
    counts, rest = [largest] + [least] * (count - 1), total - largest - least * (count - 1)
    while rest > 0:
        candidates = [i for i in range(1, count) if counts[i] < largest] or [i for i in range(1, count) if counts[i] < most]
        mass, budget = sum([portions[i] for i in candidates]), rest
        for i in candidates:
            addition = min(most - counts[i], max(1, budget * portions[i] // mass), rest)
            counts[i] = counts[i] + addition
            rest = rest - addition
    return np.array(counts)


def gaussian(own_key, dims, spread, most, shards=(), kind=jnp.bfloat16):
    loudness = level_of(own_key, dims, shards, -0.22, 0.18) if shards else 1.0
    array = jax.random.normal(own_key, dims, jnp.float32) * spread * loudness
    return jnp.minimum(jnp.maximum(array, -most), most).astype(kind)


def gaussian_with(stream_key, dims, spread, bound, cuts, heavy, kind=jnp.bfloat16):
    result = spread * jax.random.normal(stream_key, dims, jnp.float32)
    if cuts:
        result = result * level_of(stream_key, dims, cuts, -0.22, 0.18)
    return jnp.clip(raised(result, jax.random.fold_in(stream_key, 3), *heavy), -bound, bound).astype(kind)


def setup_inputs(seed: int = 0) -> dict:
    key_of = jax.random.split(jax.random.key(seed), 15)
    prompt_pool = gaussian(key_of[0], (N_ROLE, N_DP, N_EXPERT, POOL, BLK, KV), 1.0, 6.0, ((0, 2), (1, 2), (2, 64)))
    block_table = draw_block_table(jax.random.fold_in(key_of[14], 71), 0)
    cache_len = draw_cache_len(jax.random.fold_in(key_of[14], 71), 0)
    queries = draw_queries(jax.random.fold_in(key_of[14], 71), 0)
    fresh_latent = gaussian(key_of[4], (STEPS, N_ROLE, N_DP, REQ, KV), 1.0, 6.0, ((1, 2), (2, 2)))
    x_in = gaussian(key_of[5], (STEPS, N_ROLE, N_DP, REQ, D), 0.5, 4.0, ((1, 2), (2, 2), (4, 64)))
    routes_keys = jax.random.split(jax.random.fold_in(key_of[6], 1), STEPS * N_ROLE * N_DP * REQ // REQ)
    routes_turns = jax.random.permutation(jax.random.fold_in(key_of[6], 3), STEPS * N_ROLE * N_DP * REQ // REQ)
    routes = jax.vmap(lambda own, number: deal_out(jax.random.fold_in(key_of[6], 2), own, number, REQ, EXPERTS, TOP, CAP, 2))(routes_keys, routes_turns).reshape((STEPS, N_ROLE, N_DP, REQ, TOP))
    gates = jnp.clip(0.2 + 0.8 * jax.random.uniform(key_of[7], (STEPS, N_ROLE, N_DP, REQ, TOP), jnp.float32) ** level_of(key_of[7], (STEPS, N_ROLE, N_DP, REQ, TOP), ((1, 2), (2, 2)), -0.2, 0.2), 0.2, 1.0)
    norm_gain = jnp.clip(1.0 + 0.1 * jax.random.normal(key_of[8], (D,), jnp.float32), 0.5, 1.5)
    value_up = gaussian(key_of[9], (HEADS, LAT, VHEAD), LAT ** -0.5, 0.25, ((0, 64),))
    out_proj = gaussian_with(key_of[10], (HEADS * VHEAD, D), (HEADS * VHEAD) ** -0.5, 0.1875, ((0, 64),), (0, 1, 64, 4.0))
    w_gate = gaussian(key_of[11], (EXPERTS * SLICES, D, HID_DEV), D ** -0.5, 0.0625, ((0, 128),))
    w_up = gaussian(key_of[12], (EXPERTS * SLICES, D, HID_DEV), D ** -0.5, 0.0625, ((0, 128),))
    w_down = gaussian(key_of[13], (EXPERTS * SLICES, HID_DEV, D), EXP_WIDTH ** -0.5, 0.1875, ((0, 128),))
    return dict(prompt_pool=prompt_pool, block_table=block_table, cache_len=cache_len, queries=queries, fresh_latent=fresh_latent, x_in=x_in, routes=routes, gates=gates, norm_gain=norm_gain, value_up=value_up, out_proj=out_proj, w_gate=w_gate, w_up=w_up, w_down=w_down)


SCORE_SCALE = 192.0 ** (-0.5)
EPSILON = 1e-06
MASK_VALUE = -1e+30

def block_parts(queries_now, cached, lengths, offset):
    scores = jnp.einsum('qhc,qpc->qhp', queries_now.astype(jnp.float32), cached.astype(jnp.float32)) * SCORE_SCALE
    places = offset + lax.broadcasted_iota(jnp.int32, (1, 1, cached.shape[1]), 2)
    usable = places < lengths[:, None, None]
    scores = jnp.where(usable, scores, MASK_VALUE)
    maximum = lax.optimization_barrier(jnp.max(scores, axis=2))
    weights = jnp.where(usable, jnp.exp(scores - maximum[:, :, None]), 0.0)
    totals = lax.optimization_barrier(jnp.sum(weights, axis=2))
    rounded = lax.optimization_barrier(weights.astype(jnp.bfloat16)).astype(jnp.float32)
    summed = jnp.einsum('qhp,qpc->qhc', rounded, cached[:, :, :LAT].astype(jnp.float32))
    return (maximum, totals, summed)

def finish_context(maximum, totals, summed, queries_now, fresh):
    fresh_scores = jnp.einsum('qhc,tqc->qht', queries_now.astype(jnp.float32), fresh.astype(jnp.float32)) * SCORE_SCALE
    highest = jnp.maximum(maximum, lax.optimization_barrier(jnp.max(fresh_scores, axis=2)))
    carried = jnp.exp(maximum - highest)
    fresh_weights = jnp.exp(fresh_scores - highest[:, :, None])
    rounded = lax.optimization_barrier(fresh_weights.astype(jnp.bfloat16)).astype(jnp.float32)
    numerator = carried[:, :, None] * summed + jnp.einsum('qht,tqc->qhc', rounded, fresh[:, :, :LAT].astype(jnp.float32))
    denominator = carried * totals + lax.optimization_barrier(jnp.sum(fresh_weights, axis=2))
    return (numerator / denominator[:, :, None]).astype(jnp.bfloat16)

def group_outputs(pool_source, tables, lengths, queries_g, fresh_g, x_g, routes_g, gates_g, norm_gain, value_up, out_proj, gate_full, up_full, down_full):
    span = NBLK * BLK

    def gather_block(index):
        rows = jnp.take(pool_source[index], tables[index].reshape(-1), axis=0)
        return rows.reshape(REQ, span, KV)
    cached_all = lax.map(gather_block, jnp.arange(N_EXPERT, dtype=jnp.int32))
    expert_ids = jnp.arange(EXPERTS, dtype=jnp.int32)
    results = []
    for step_index in range(STEPS):
        queries_now = queries_g[step_index]

        def one_block(index):
            return block_parts(queries_now, cached_all[index], lengths, (index * span).astype(jnp.int32))
        maxima, totals, summed = lax.map(one_block, jnp.arange(N_EXPERT, dtype=jnp.int32))
        overall = lax.optimization_barrier(jnp.max(maxima, axis=0))
        factors = jnp.exp(maxima - overall[None])
        totals_all = lax.optimization_barrier(jnp.sum(factors * totals, axis=0))
        summed_all = lax.optimization_barrier(jnp.sum(factors[..., None] * summed, axis=0))
        context = finish_context(overall, totals_all, summed_all, queries_now, fresh_g[:step_index + 1])
        head_vals = jnp.einsum('qhl,hlv->qhv', context.astype(jnp.float32), value_up.astype(jnp.float32)).astype(jnp.bfloat16)
        attended = jnp.dot(head_vals.reshape(REQ, HEADS * VHEAD), out_proj, preferred_element_type=jnp.float32)
        resid = (x_g[step_index].astype(jnp.float32) + attended).astype(jnp.bfloat16)
        flat = resid.astype(jnp.float32)
        normed = (flat * lax.rsqrt(lax.optimization_barrier(jnp.mean(flat * flat, axis=1, keepdims=True)) + EPSILON) * norm_gain).astype(jnp.bfloat16)

        def one_expert(index):
            gate_part = jnp.dot(normed, gate_full[index], preferred_element_type=jnp.float32)
            up_part = jnp.dot(normed, up_full[index], preferred_element_type=jnp.float32)
            hidden_act = (jax.nn.silu(gate_part) * up_part).astype(jnp.bfloat16)
            return jnp.dot(hidden_act, down_full[index], preferred_element_type=jnp.float32)
        expert_rows = lax.map(one_expert, expert_ids)
        chosen = (routes_g[step_index][:, :, None] == expert_ids[None, None, :]).astype(jnp.float32)
        mixing = lax.optimization_barrier(jnp.sum(gates_g[step_index][:, :, None] * chosen, axis=1))
        mixed = jnp.einsum('qx,xqf->qf', mixing, expert_rows, precision=lax.Precision.HIGHEST)
        results.append((flat + mixed).astype(jnp.bfloat16))
    return jnp.stack(results)

def reference(prompt_pool, block_table, cache_len, queries, fresh_latent, x_in, routes, gates, norm_gain, value_up, out_proj, w_gate, w_up, w_down):
    gate_full = w_gate.reshape(EXPERTS, SLICES, D, HID_DEV).transpose(0, 2, 1, 3).reshape(EXPERTS, D, EXP_WIDTH)
    up_full = w_up.reshape(EXPERTS, SLICES, D, HID_DEV).transpose(0, 2, 1, 3).reshape(EXPERTS, D, EXP_WIDTH)
    down_full = w_down.reshape(EXPERTS, EXP_WIDTH, D)
    per_role = []
    for role_index in range(N_ROLE):
        per_dp = []
        for dp_index in range(N_DP):
            per_dp.append(group_outputs(prompt_pool[1 - role_index, dp_index], block_table[role_index, dp_index], cache_len[role_index, dp_index], queries[:, role_index, dp_index], fresh_latent[:, role_index, dp_index], x_in[:, role_index, dp_index], routes[:, role_index, dp_index], gates[:, role_index, dp_index], norm_gain, value_up, out_proj, gate_full, up_full, down_full))
        per_role.append(jnp.stack(per_dp, axis=1))
    return jnp.stack(per_role, axis=1)
```

```python
import jax
import jax.numpy as jnp
from jax import lax
from jax.experimental import pallas as pl
from jax.experimental.pallas import tpu as pltpu
from jax.sharding import Mesh, PartitionSpec as P

SCORE_SCALE = 192.0 ** (-0.5)
EPSILON = 1e-06
MASK_VALUE = -1e30
SLICES = 8
CHIPS = 32
HALF = 3584
CHUNKS = 28
BLOCK = 112
XZ = ("x", "z")
DXZ = ("dp", "x", "z")
bf16 = jnp.bfloat16
f32 = jnp.float32


def swap(value, axis):
    return lax.ppermute(value, axis, [(0, 1), (1, 0)])


def exchange(value, axes):
    return lax.all_to_all(value, axes, 0, 0, tiled=True)


def pieces(value):
    first = value.astype(bf16)
    rest = value - first.astype(f32)
    second = rest.astype(bf16)
    third = (rest - second.astype(f32)).astype(bf16)
    return first, second, third


VM = pl.BlockSpec(memory_space=pltpu.VMEM)
SM = pl.BlockSpec(memory_space=pltpu.SMEM)
LIMIT = 32 * 1024 * 1024


def pick_kernel(ids, queries, out):
    row = lax.broadcasted_iota(jnp.int32, (32, 64), 0)
    col = lax.broadcasted_iota(jnp.int32, (32, 64), 1)
    wanted = jnp.where(col == 2 * row + ids[0], 1.0, 0.0).astype(bf16)
    for i in range(8):
        out[i] = jnp.dot(wanted, queries[i], preferred_element_type=f32).astype(bf16)


def pick_heads(ids, queries):
    return pl.pallas_call(
        pick_kernel,
        out_shape=jax.ShapeDtypeStruct((8, 32, 576), bf16),
        in_specs=[SM, VM],
        out_specs=VM,
        compiler_params=pltpu.CompilerParams(vmem_limit_bytes=LIMIT),
        cost_estimate=pl.CostEstimate(flops=19000000, bytes_accessed=900000, transcendentals=0),
    )(ids, queries)


def attention_kernel(ids, table, table_other, lengths, q, pool, pool_other, out, scratch):
    wanted = ids[1]
    place = ids[2]
    lane = lax.broadcasted_iota(jnp.int32, (1, 512), 1)
    start = jnp.where(lane < 256, place * 256, ((place + 1 - 2 * ids[0]) - 1) * 256)
    places = start + lane
    slot = lax.broadcasted_iota(jnp.int32, (32, 128), 1)
    for r in range(4):
        blocks = [pool[table[wanted, r, j]] for j in range(4)]
        blocks += [pool_other[table_other[wanted, r, j]] for j in range(4)]
        keys = jnp.concatenate(blocks, axis=0)
        asked = jnp.concatenate([q[r], q[4 + r]], axis=0)
        scores = lax.dot_general(
            asked, keys, (((1,), (1,)), ((), ())), preferred_element_type=f32
        )
        usable = places < lengths[r]
        scores = jnp.where(usable, scores * SCORE_SCALE, MASK_VALUE)
        top = jnp.max(scores, axis=1, keepdims=True)
        weights = jnp.where(usable, jnp.exp(scores - top), 0.0)
        total = jnp.sum(weights, axis=1, keepdims=True)
        summed = jnp.dot(weights.astype(bf16), keys[:, :512], preferred_element_type=f32)
        live = total > 0.0
        safe = jnp.where(live, total, 1.0)
        level = jnp.where(live, top + jnp.log(safe), MASK_VALUE)
        value = summed * (1.0 / safe)
        first = level.astype(bf16).astype(f32)
        second = (level - first).astype(bf16).astype(f32)
        third = (level - first) - second
        for s in range(2):
            rows = slice(32 * s, 32 * s + 32)
            tail = jnp.where(
                slot == 0,
                first[rows],
                jnp.where(slot == 1, second[rows], jnp.where(slot == 2, third[rows], 0.0)),
            )
            for k in range(5):
                part = value[rows, 128 * k : 128 * k + 128] if k < 4 else tail
                scratch[k, pl.ds(4 * s + r, 32, stride=8), :] = part
    for k in range(5):
        out[:, :, 128 * k : 128 * k + 128] = scratch[k].reshape(32, 8, 128).astype(bf16)


def attend(ids, table, table_other, lengths, q, pool, pool_other):
    return pl.pallas_call(
        attention_kernel,
        out_shape=jax.ShapeDtypeStruct((32, 8, 640), bf16),
        in_specs=[SM, SM, SM, SM, VM, VM, VM],
        out_specs=VM,
        scratch_shapes=[pltpu.VMEM((5, 256, 128), f32)],
        compiler_params=pltpu.CompilerParams(vmem_limit_bytes=LIMIT),
        cost_estimate=pl.CostEstimate(
            flops=300000000, bytes_accessed=4000000, transcendentals=131072
        ),
    )(ids, table, table_other, lengths, q, pool, pool_other)


def body(
    prompt_pool,
    block_table,
    cache_len,
    queries,
    fresh_latent,
    x_in,
    routes,
    gates,
    norm_gain,
    value_up,
    out_proj,
    w_gate,
    w_up,
    w_down,
):
    role = lax.axis_index("role")
    dp = lax.axis_index("dp")
    core = lax.axis_index("core")
    chip = lax.axis_index("x") * lax.axis_size("z") + lax.axis_index("z")
    place = chip * 2 + core
    ids = jnp.stack([core, 1 - role, place]).astype(jnp.int32)
    q = swap(pick_heads(ids, queries.reshape(8, 64, 576)), "role")
    fresh = swap(fresh_latent.reshape(2, 4, 576), "role")
    x_here = swap(x_in.reshape(8, BLOCK), "role")
    routes_now = swap(routes.reshape(8, 8), "role")
    gates_now = swap(gates.reshape(8, 8), "role")
    lengths = swap(cache_len.reshape(4), "role")
    pool = prompt_pool[0, 0, 0]
    pool_other = swap(pool, "core")
    table = block_table[:, 0, 0]
    table_other = swap(table, "core")
    x_other = swap(x_here, "core")
    proj_other = swap(
        lax.dynamic_slice_in_dim(out_proj, (1 - core) * HALF, HALF, 1), "core"
    )
    proj_mine = lax.dynamic_slice_in_dim(out_proj, core * HALF, HALF, 1)
    down_mine = w_down[0]
    down_other = swap(down_mine, "core")
    sent = attend(ids, table, table_other, lengths, q, pool, pool_other)
    got = exchange(sent, XZ)
    levels = jnp.sum(got[:, :, 512:515].astype(f32), axis=2, keepdims=True)
    q_mine = lax.dynamic_index_in_dim(q, chip, 1, keepdims=False).reshape(2, 4, 576)
    fresh_scores = (
        jnp.einsum("sqc,tqc->sqt", q_mine, fresh, preferred_element_type=f32) * SCORE_SCALE
    )
    fresh_usable = (jnp.arange(2)[None, :] <= jnp.arange(2)[:, None])[:, None, :]
    fresh_scores = jnp.where(fresh_usable, fresh_scores, MASK_VALUE)
    highest = jnp.maximum(
        jnp.max(levels, axis=0).reshape(2, 4, 1), jnp.max(fresh_scores, axis=2, keepdims=True)
    )
    factors = jnp.exp(levels - highest.reshape(1, 8, 1))
    fresh_weights = jnp.where(fresh_usable, jnp.exp(fresh_scores - highest), 0.0)
    numerator = jnp.sum(factors * got[:, :, :512].astype(f32), axis=0).reshape(2, 4, 512)
    numerator = numerator + jnp.einsum(
        "sqt,tqc->sqc", fresh_weights.astype(bf16), fresh[:, :, :512], preferred_element_type=f32
    )
    denominator = jnp.sum(factors, axis=0).reshape(2, 4, 1) + jnp.sum(
        fresh_weights, axis=2, keepdims=True
    )
    context = (numerator / denominator).astype(bf16).reshape(8, 512)
    head_vals = jnp.dot(context, value_up[0], preferred_element_type=f32).astype(bf16)
    vals_other = swap(head_vals, "core")
    base = jnp.zeros((8, 2 * HALF), bf16)
    base = lax.dynamic_update_slice_in_dim(base, x_here, place * BLOCK, 1)
    base = lax.dynamic_update_slice_in_dim(base, x_other, (place + 1 - 2 * core) * BLOCK, 1)
    base = lax.dynamic_slice_in_dim(base, core * HALF, HALF, 1)
    partial = (
        base.astype(f32)
        + jnp.dot(head_vals, proj_mine, preferred_element_type=f32)
        + jnp.dot(vals_other, proj_other, preferred_element_type=f32)
    ).astype(bf16)
    partial = jnp.pad(partial.reshape(8, CHUNKS, 128).transpose(1, 0, 2), ((0, 4), (0, 0), (0, 0)))
    resid_piece = jnp.sum(exchange(partial, XZ).astype(f32), axis=0).astype(bf16)
    rows_half = exchange(jnp.broadcast_to(resid_piece[None], (64, 8, 128)), DXZ)
    rows_other = swap(rows_half, "core")
    first = jnp.where(core == 0, rows_half, rows_other)
    second = jnp.where(core == 0, rows_other, rows_half)
    rows = jnp.stack([first, second]).reshape(2, 2, 32, 8, 128)[:, :, :CHUNKS]
    rows = rows.transpose(1, 3, 0, 2, 4).reshape(16, 2 * HALF)
    flat = rows.astype(f32)
    normed = (
        flat * lax.rsqrt(jnp.mean(flat * flat, axis=1, keepdims=True) + EPSILON) * norm_gain
    ).astype(bf16)
    gate_part = jnp.dot(normed, w_gate[0], preferred_element_type=f32)
    up_part = jnp.dot(normed, w_up[0], preferred_element_type=f32)
    hidden = (jax.nn.silu(gate_part) * up_part).astype(bf16)
    hidden_other = swap(hidden, "core")
    out_rows = jnp.dot(hidden, down_mine, preferred_element_type=f32) + jnp.dot(
        hidden_other, down_other, preferred_element_type=f32
    )
    expert = dp * 8 + chip // 4
    mixing_mine = jnp.sum(jnp.where(routes_now == expert, gates_now, 0.0), axis=1, keepdims=True)
    mixing_theirs = swap(
        jnp.sum(jnp.where(routes_now == (1 - dp) * 8 + chip // 4, gates_now, 0.0), axis=1, keepdims=True),
        "dp",
    )
    mixing = jnp.where(
        dp == 0,
        jnp.concatenate([mixing_mine, mixing_theirs]),
        jnp.concatenate([mixing_theirs, mixing_mine]),
    )
    out_rows = (out_rows * mixing).astype(bf16)
    outgoing = lax.dynamic_index_in_dim(out_rows.reshape(2, 8, 32, 2, BLOCK), core, 3, keepdims=False)
    outgoing = outgoing.transpose(0, 2, 1, 3).reshape(64, 8, BLOCK)
    back = jnp.sum(exchange(outgoing, DXZ).astype(f32), axis=0)
    own_rows = lax.dynamic_slice_in_dim(rows, dp * 8, 8, 0)
    own = lax.dynamic_slice_in_dim(own_rows, place * BLOCK, BLOCK, 1).astype(f32)
    done = swap((own + back).astype(bf16), "role")
    return done.reshape(2, 1, 1, 4, BLOCK)


def solution(mesh):
    split = Mesh(mesh.devices.reshape(2, 2, 4, 8, 2), ("role", "dp", "x", "z", "core"))
    e = ("x", "z", "core")
    slab = ("dp", "x", "z", "core")
    placed = (
        P("role", "dp", e, None, None, None),
        P(None, "dp", e, None, None),
        P("role", "dp", None),
        P(None, "role", "dp", None, None, None),
        P(None, "role", "dp", None, None),
        P(None, "role", "dp", None, e),
        P(None, "role", "dp", None, None),
        P(None, "role", "dp", None, None),
        P(),
        P(e, None, None),
        P(e, None),
        P(slab, None, None),
        P(slab, None, None),
        P(slab, None, None),
    )
    return jax.shard_map(
        body,
        mesh=split,
        in_specs=placed,
        out_specs=P(None, "role", "dp", None, e),
        check_vma=False,
    )
```

```python
import jax
import jax.numpy as jnp
from jax import lax
from jax.experimental import pallas as pl
from jax.experimental.pallas import tpu as pltpu
from jax.sharding import Mesh, PartitionSpec as P

SCORE_SCALE = 192.0 ** (-0.5)
EPSILON = 1e-06
MASK_VALUE = -1e30
HALF = 3584
CHUNKS = 28
BLOCK = 112
XZ = ("x", "z")
DXZ = ("dp", "x", "z")
bf16 = jnp.bfloat16
f32 = jnp.float32

VM = pl.BlockSpec(memory_space=pltpu.VMEM)
SM = pl.BlockSpec(memory_space=pltpu.SMEM)
ANY = pl.BlockSpec(memory_space=pl.ANY)
FAR = pl.BlockSpec(memory_space=pltpu.HBM)
MIB = 1024 * 1024


def call(kernel, outs, specs, args, flops, moved, scratch=(), limit=16, exps=0):
    many = isinstance(outs, list)
    return pl.pallas_call(
        kernel,
        out_shape=outs,
        in_specs=specs,
        out_specs=[VM] * len(outs) if many else VM,
        scratch_shapes=list(scratch),
        compiler_params=pltpu.CompilerParams(vmem_limit_bytes=limit * MIB),
        cost_estimate=pl.CostEstimate(flops=flops, bytes_accessed=moved, transcendentals=exps),
    )(*args)


def shape(*dims, dtype=bf16):
    return jax.ShapeDtypeStruct(dims, dtype)


def far(value):
    return pltpu.with_memory_space_constraint(value, pltpu.HBM)


def swap(value, axis):
    return lax.ppermute(value, axis, [(0, 1), (1, 0)])


def exchange(value, axes):
    return lax.all_to_all(value, axes, 0, 0, tiled=True)


def split(value):
    first = value.astype(bf16).astype(f32)
    second = (value - first).astype(bf16).astype(f32)
    return first, second, (value - first) - second


def pick_kernel(ids, *refs):
    sources, pool, (out, keys), landed, (wide, sems) = refs[:7], refs[7], refs[8:10], refs[10:17], refs[17:]
    copies = [
        pltpu.make_async_copy(
            sources[0].at[pl.ds(2 * i, 2)], landed[0].at[pl.ds(2 * i, 2)], sems.at[i]
        )
        for i in range(4)
    ] + [pltpu.make_async_copy(sources[i], landed[i], sems.at[3 + i]) for i in range(1, 7)]
    for one in copies:
        one.start()
    queries, fresh, x_in, routes, gates, lengths, table = landed
    copies[9].wait()
    gathered = [
        pltpu.make_async_copy(
            pool.at[table[ids[1], i // 4, i % 4]], keys.at[i], sems.at[10 + i]
        )
        for i in range(16)
    ]
    for one in gathered:
        one.start()
    for i in range(8):
        if i % 2 == 0:
            copies[i // 2].wait()
        asked = queries[i].astype(f32)
        for k in range(5):
            lanes = slice(128 * k, min(128 * k + 128, 576))
            wide[k, 64 * i : 64 * i + 64, 0 : lanes.stop - lanes.start] = asked[:, lanes]
        for k in range(5):
            lanes = slice(128 * k, min(128 * k + 128, 576))
            half = wide[k, pl.ds(64 * i + ids[0], 32, stride=2), :]
            out[i, :, lanes] = half[:, 0 : lanes.stop - lanes.start].astype(bf16)
    lane = lax.broadcasted_iota(jnp.int32, (4, 128), 1)
    for one in copies[4:9]:
        one.wait()
    count = jnp.concatenate([lengths[...], jnp.zeros((1, 124), jnp.int32)], axis=1)
    high = lax.shift_right_logical(count, 7)
    told = pltpu.roll(high.astype(f32), 64, 1) + pltpu.roll((count - 128 * high).astype(f32), 68, 1)
    rows = []
    blocks = []
    for s in range(2):
        note = jnp.zeros((4, 128), f32)
        for k in range(8):
            note = note + jnp.where(lane == routes[s][:, k : k + 1], gates[s][:, k : k + 1], 0.0)
        parts = split(note)
        note = parts[0] + pltpu.roll(parts[1], 16, 1) + pltpu.roll(parts[2], 32, 1) + told
        rows.append(fresh[s].astype(f32))
        block = jnp.concatenate([x_in[s].astype(f32), jnp.zeros((4, 16), f32)], axis=1)
        blocks.append(jnp.concatenate([block, note, jnp.zeros((4, 320), f32)], axis=1))
    blank = [jnp.zeros((8, 576), f32)]
    out[8] = jnp.concatenate(rows + blank + blocks + blank, axis=0).astype(bf16)
    for one in gathered:
        one.wait()


def attention_kernel(ids, q, keys_mine, keys_other, *rest):
    out, told, scratch = rest[-3:]
    lane = lax.broadcasted_iota(jnp.int32, (1, 512), 1)
    start = jnp.where(lane < 256, ids[2] * 256, (ids[2] - 2 * ids[0]) * 256)
    places = (start + lane).astype(f32)
    slot = lax.broadcasted_iota(jnp.int32, (32, 128), 1)
    extra = q[8]
    notes = extra[16:32, 128:256].astype(f32)
    told[0:8, :] = extra[16:32, 0:128].astype(f32)[0:8]
    told[8:16, :] = notes[0:8]
    fresh = extra[0:16]
    row = lax.broadcasted_iota(jnp.int32, (64, 16), 0)
    col = lax.broadcasted_iota(jnp.int32, (64, 16), 1)
    for r in range(4):
        keys = jnp.concatenate(
            [side[4 * r + j] for side in (keys_mine, keys_other) for j in range(4)], axis=0
        )
        asked = jnp.concatenate([q[r], q[4 + r]], axis=0)
        scores = lax.dot_general(
            asked, keys, (((1,), (1,)), ((), ())), preferred_element_type=f32
        )
        late = lax.dot_general(
            asked, fresh, (((1,), (1,)), ((), ())), preferred_element_type=f32
        )
        usable = places < notes[0:1, 64 + r : 65 + r] * 128.0 + notes[0:1, 68 + r : 69 + r]
        counted = (ids[3] == 0) & ((col == r) | ((col == 4 + r) & (row >= 32)))
        scores = jnp.where(usable, scores * SCORE_SCALE, MASK_VALUE)
        late = jnp.where(counted, late * SCORE_SCALE, MASK_VALUE)
        top = jnp.maximum(
            jnp.max(scores, axis=1, keepdims=True), jnp.max(late, axis=1, keepdims=True)
        )
        weights = jnp.where(usable, jnp.exp(scores - top), 0.0)
        late = jnp.where(counted, jnp.exp(late - top), 0.0)
        total = jnp.sum(weights, axis=1, keepdims=True) + jnp.sum(late, axis=1, keepdims=True)
        summed = jnp.dot(weights.astype(bf16), keys[:, :512], preferred_element_type=f32)
        summed = summed + jnp.dot(
            late.astype(bf16), fresh[:, :512], preferred_element_type=f32
        )
        live = total > 0.0
        safe = jnp.where(live, total, 1.0)
        level = jnp.where(live, top + jnp.log(safe), MASK_VALUE)
        value = summed * (1.0 / safe)
        first, second, third = split(level)
        for s in range(2):
            rows = slice(32 * s, 32 * s + 32)
            tail = jnp.where(
                slot == 0,
                first[rows],
                jnp.where(slot == 1, second[rows], jnp.where(slot == 2, third[rows], 0.0)),
            )
            for k in range(5):
                part = value[rows, 128 * k : 128 * k + 128] if k < 4 else tail
                scratch[k, pl.ds(4 * s + r, 32, stride=8), :] = part
    for k in range(5):
        out[:, :, 128 * k : 128 * k + 128] = scratch[k].reshape(32, 8, 128).astype(bf16)


def context_kernel(ids, got, told, value_up, proj, kept, sent):
    level = jnp.sum(got[:, :, 512:640].astype(f32), axis=2, keepdims=True)
    factors = jnp.exp(level - jnp.max(level, axis=0, keepdims=True))
    denominator = jnp.sum(factors, axis=0)
    numerator = jnp.zeros((8, 512), f32)
    for i in range(32):
        numerator = numerator + factors[i] * got[i, :, 0:512].astype(f32)
    context = (numerator / denominator).astype(bf16)
    vals = jnp.dot(context, value_up[...], preferred_element_type=f32).astype(bf16)
    start = jnp.concatenate([told[0:8, :], jnp.zeros((8, HALF - 128), f32)], axis=1)
    start = pltpu.roll(start, (ids[2] % 32) * BLOCK, 1)
    for out, half in ((sent, 1 - ids[0]), (kept, ids[0])):
        lanes = pl.ds(pl.multiple_of(half * HALF, 128), HALF)
        total = jnp.dot(vals, proj[:, lanes], preferred_element_type=f32)
        total = total + jnp.where(ids[2] // 32 == half, start, 0.0)
        for k in range(CHUNKS):
            out[k] = total[:, 128 * k : 128 * k + 128].astype(out.dtype)


def join_kernel(kept, other, out):
    for k in range(CHUNKS):
        out[k] = (kept[k] + other[k].astype(f32)).astype(bf16)
    for k in range(CHUNKS, 32):
        out[k] = jnp.zeros((8, 128), bf16)


def spread_kernel(ids, got, told, out):
    total = got[0].astype(f32)
    for i in range(1, 32):
        total = total + got[i].astype(f32)
    piece = jnp.where(ids[3] == CHUNKS, told[8:16, :], total).astype(bf16)
    for i in range(64):
        out[i] = piece


def raise_kernel(ids, rows, gain, gate, up, gate_other, up_other, out, scaled, own):
    squares = [jnp.zeros((8, 128), f32) for _ in range(2)]
    for k in range(CHUNKS):
        lanes = slice(128 * k, 128 * k + 128)
        parts = [rows[32 * d + k].astype(f32) for d in range(2)]
        squares = [squares[d] + parts[d] * parts[d] for d in range(2)]
        both = jnp.concatenate(parts, axis=0) * gain[pl.ds(ids[0] * CHUNKS + k, 1), :]
        scaled[:, lanes] = both.astype(bf16)
        own[:, lanes] = jnp.where(ids[4] == 0, parts[0], parts[1])
    here = pl.ds(pl.multiple_of(ids[0] * HALF, 128), HALF)
    asked = scaled[...]
    out[:, 0:128] = jnp.dot(asked, gate[here, :], preferred_element_type=f32)
    out[:, 128:256] = jnp.dot(asked, up[here, :], preferred_element_type=f32)
    out[:, 256:384] = jnp.dot(asked, gate_other[here, :], preferred_element_type=f32)
    out[:, 384:512] = jnp.dot(asked, up_other[here, :], preferred_element_type=f32)
    out[:, 512:640] = jnp.concatenate(squares, axis=0)
    shift = HALF - (ids[3] % 16) * (2 * BLOCK)
    turned = pltpu.roll(own[...], shift, 1)[:, 0:256]
    out[0:8, 640:896] = jnp.where(ids[0] == ids[3] // 16, turned, 0.0)
    out[8:16, 640:896] = jnp.zeros((8, 256), f32)


def lower_kernel(ids, mine, other, rows, down, down_other, out, own, product):
    squares = jnp.sum(mine[:, 512:640] + other[:, 512:640], axis=1, keepdims=True)
    scale = lax.rsqrt(squares * (1.0 / (2 * HALF)) + EPSILON)

    def active(near, near_at, far, far_at):
        gate = (near[:, near_at : near_at + 128] + far[:, far_at : far_at + 128]) * scale
        up = (
            near[:, near_at + 128 : near_at + 256] + far[:, far_at + 128 : far_at + 256]
        ) * scale
        return (gate / (1.0 + jnp.exp(-gate)) * up).astype(bf16)

    told = jnp.concatenate([rows[CHUNKS].astype(f32), rows[32 + CHUNKS].astype(f32)], axis=0)
    lane = lax.broadcasted_iota(jnp.int32, (16, 128), 1)
    wanted = (lane % 16 == ids[4] * 8 + ids[3] // 4) & (lane < 48)
    mixing = jnp.sum(jnp.where(wanted, told, 0.0), axis=1, keepdims=True)
    here = active(mine, 0, other, 256)
    there = active(other, 0, mine, 256)
    for k in range(14):
        lanes = slice(512 * k, 512 * k + 512)
        total = jnp.dot(here, down[:, lanes], preferred_element_type=f32)
        total = total + jnp.dot(there, down_other[:, lanes], preferred_element_type=f32)
        product[:, lanes] = total * mixing
    product[:, 7168:7296] = jnp.zeros((16, 128), f32)
    both = mine[0:8, 640:896] + other[0:8, 640:896]

    def fill(core):
        for k in range(32):
            at = (2 * k + core) * BLOCK
            base, turn = at // 128 * 128, at % 128
            for d in range(2):
                part = product[8 * d : 8 * d + 8, base : base + 256]
                if turn:
                    part = pltpu.roll(part, 256 - turn, 1)
                out[32 * d + k] = part[:, 0:128].astype(bf16)
        part = pltpu.roll(both, 256 - BLOCK, 1) if core else both
        own[...] = part[:, 0:128]

    @pl.when(ids[0] == 0)
    def _():
        fill(0)

    @pl.when(ids[0] == 1)
    def _():
        fill(1)


def finish_kernel(got, own, out):
    total = own[...]
    for i in range(64):
        total = total + got[i].astype(f32)
    for s in range(2):
        out[s] = total[4 * s : 4 * s + 4, 0:BLOCK].astype(bf16)


def body(
    prompt_pool,
    block_table,
    cache_len,
    queries,
    fresh_latent,
    x_in,
    routes,
    gates,
    norm_gain,
    value_up,
    out_proj,
    w_gate,
    w_up,
    w_down,
):
    role = lax.axis_index("role")
    dp = lax.axis_index("dp")
    core = lax.axis_index("core")
    chip = lax.axis_index("x") * lax.axis_size("z") + lax.axis_index("z")
    ids = jnp.stack([core, 1 - role, chip * 2 + core, chip, dp]).astype(jnp.int32)
    half_there = (1 - core) * HALF
    gate_other, up_other, down_other = [
        swap(one, "core") for one in (w_gate[0], w_up[0], w_down[0])
    ]
    given = (
        queries.reshape(8, 64, 576),
        fresh_latent.reshape(2, 4, 576),
        x_in.reshape(2, 4, BLOCK),
        routes.reshape(2, 4, 8),
        gates.reshape(2, 4, 8),
        cache_len.reshape(1, 4),
        block_table[:, 0, 0],
    )
    picked, keys = call(
        pick_kernel,
        [shape(9, 32, 576), shape(16, 64, 576)],
        [SM] + [FAR] * 8,
        (ids,) + tuple(far(one) for one in given + (prompt_pool[0, 0, 0],)),
        19000000,
        900000,
        [pltpu.VMEM(one.shape, one.dtype) for one in given[:6]]
        + [pltpu.SMEM((2, 4, 4), jnp.int32), pltpu.VMEM((5, 512, 128), f32)]
        + [pltpu.SemaphoreType.DMA((26,))],
        8,
    )
    q = swap(picked, "role")
    keys_other = swap(keys, "core")
    after = (gate_other, up_other, down_other)[:EXTRA]
    sent, told = call(
        attention_kernel,
        [shape(32, 8, 640), shape(16, 128, dtype=f32)],
        [SM, VM, VM, VM] + [ANY] * len(after),
        (ids, q, keys, keys_other) + after,
        300000000,
        4000000,
        [pltpu.VMEM((5, 256, 128), f32)],
        16,
        131072,
    )
    got = exchange(sent, XZ)
    kept, passed = call(
        context_kernel,
        [shape(CHUNKS, 8, 128, dtype=f32), shape(CHUNKS, 8, 128)],
        [SM] + [VM] * 4,
        (ids, got, told, value_up[0], out_proj),
        20000000,
        2500000,
        (),
        8,
    )
    partial = call(
        join_kernel, shape(32, 8, 128), [VM] * 2, (kept, swap(passed, "core")), 30000, 200000, (), 4
    )
    rows = exchange(
        call(
            spread_kernel,
            shape(64, 8, 128),
            [SM, VM, VM],
            (ids, exchange(partial, XZ), told),
            40000,
            200000,
            (),
            4,
        ),
        DXZ,
    )
    raised = call(
        raise_kernel,
        shape(16, 896, dtype=f32),
        [SM] + [VM] * 6,
        (ids, rows, norm_gain.reshape(56, 128), w_gate[0], w_up[0], gate_other, up_other),
        60000000,
        6000000,
        [pltpu.VMEM((16, HALF), bf16), pltpu.VMEM((8, HALF), f32)],
        16,
    )
    raised_other = swap(raised, "core")
    outgoing, own = call(
        lower_kernel,
        [shape(64, 8, 128), shape(8, 128, dtype=f32)],
        [SM] + [VM] * 5,
        (ids, raised, raised_other, rows, w_down[0], down_other),
        60000000,
        4000000,
        [pltpu.VMEM((16, 7296), f32)],
        16,
        4096,
    )
    done = call(
        finish_kernel, shape(2, 4, BLOCK), [VM] * 2, (exchange(outgoing, DXZ), own), 70000, 140000, (), 4
    )
    return swap(done, "role").reshape(2, 1, 1, 4, BLOCK)


EXTRA = 6


def solution(mesh):
    split = Mesh(mesh.devices.reshape(2, 2, 4, 8, 2), ("role", "dp", "x", "z", "core"))
    e = ("x", "z", "core")
    slab = ("dp", "x", "z", "core")
    placed = (
        P("role", "dp", e, None, None, None),
        P(None, "dp", e, None, None),
        P("role", "dp", None),
        P(None, "role", "dp", None, None, None),
        P(None, "role", "dp", None, None),
        P(None, "role", "dp", None, e),
        P(None, "role", "dp", None, None),
        P(None, "role", "dp", None, None),
        P(),
        P(e, None, None),
        P(e, None),
        P(slab, None, None),
        P(slab, None, None),
        P(slab, None, None),
    )
    return jax.shard_map(
        body,
        mesh=split,
        in_specs=placed,
        out_specs=P(None, "role", "dp", None, e),
        check_vma=False,
    )
```

```python
import jax
import jax.numpy as jnp
from jax import lax
from jax.experimental import pallas as pl
from jax.experimental.pallas import tpu as pltpu
from jax.sharding import Mesh, PartitionSpec as P

SCORE_SCALE = 192.0 ** (-0.5)
EPSILON = 1e-06
MASK_VALUE = -1e30
HALF = 3584
CHUNKS = 28
BLOCK = 112
XZ = ("x", "z")
DXZ = ("dp", "x", "z")
bf16 = jnp.bfloat16
f32 = jnp.float32

VM = pl.BlockSpec(memory_space=pltpu.VMEM)
SM = pl.BlockSpec(memory_space=pltpu.SMEM)
ANY = pl.BlockSpec(memory_space=pl.ANY)
FAR = pl.BlockSpec(memory_space=pltpu.HBM)
MIB = 1024 * 1024


def call(kernel, outs, specs, args, flops, moved, scratch=(), limit=16, exps=0):
    many = isinstance(outs, list)
    return pl.pallas_call(
        kernel,
        out_shape=outs,
        in_specs=specs,
        out_specs=[VM] * len(outs) if many else VM,
        scratch_shapes=list(scratch),
        compiler_params=pltpu.CompilerParams(vmem_limit_bytes=limit * MIB),
        cost_estimate=pl.CostEstimate(flops=flops, bytes_accessed=moved, transcendentals=exps),
    )(*args)


def shape(*dims, dtype=bf16):
    return jax.ShapeDtypeStruct(dims, dtype)


def far(value):
    return pltpu.with_memory_space_constraint(value, pltpu.HBM)


def swap(value, axis):
    return lax.ppermute(value, axis, [(0, 1), (1, 0)])


def exchange(value, axes):
    return lax.all_to_all(value, axes, 0, 0, tiled=True)


def split(value):
    first = value.astype(bf16).astype(f32)
    second = (value - first).astype(bf16).astype(f32)
    return first, second, (value - first) - second


def pick_kernel(ids, *refs):
    sources, pool, (out, keys), landed, (wide, sems) = refs[:7], refs[7], refs[8:10], refs[10:17], refs[17:]
    copies = [
        pltpu.make_async_copy(
            sources[0].at[pl.ds(2 * i, 2)], landed[0].at[pl.ds(2 * i, 2)], sems.at[i]
        )
        for i in range(4)
    ] + [pltpu.make_async_copy(sources[i], landed[i], sems.at[3 + i]) for i in range(1, 7)]
    for one in copies:
        one.start()
    queries, fresh, x_in, routes, gates, lengths, table = landed
    copies[9].wait()
    gathered = [
        pltpu.make_async_copy(
            pool.at[table[ids[1], i // 4, i % 4]], keys.at[i], sems.at[10 + i]
        )
        for i in range(16)
    ]
    for one in gathered:
        one.start()
    for i in range(8):
        if i % 2 == 0:
            copies[i // 2].wait()
        asked = queries[i].astype(f32)
        for k in range(5):
            lanes = slice(128 * k, min(128 * k + 128, 576))
            wide[k, 64 * i : 64 * i + 64, 0 : lanes.stop - lanes.start] = asked[:, lanes]
        for k in range(5):
            lanes = slice(128 * k, min(128 * k + 128, 576))
            half = wide[k, pl.ds(64 * i + ids[0], 32, stride=2), :]
            out[i, :, lanes] = half[:, 0 : lanes.stop - lanes.start].astype(bf16)
    lane = lax.broadcasted_iota(jnp.int32, (4, 128), 1)
    for one in copies[4:9]:
        one.wait()
    count = jnp.concatenate([lengths[...], jnp.zeros((1, 124), jnp.int32)], axis=1)
    high = lax.shift_right_logical(count, 7)
    told = pltpu.roll(high.astype(f32), 64, 1) + pltpu.roll((count - 128 * high).astype(f32), 68, 1)
    rows = []
    blocks = []
    for s in range(2):
        note = jnp.zeros((4, 128), f32)
        for k in range(8):
            note = note + jnp.where(lane == routes[s][:, k : k + 1], gates[s][:, k : k + 1], 0.0)
        parts = split(note)
        note = parts[0] + pltpu.roll(parts[1], 16, 1) + pltpu.roll(parts[2], 32, 1) + told
        rows.append(fresh[s].astype(f32))
        block = jnp.concatenate([x_in[s].astype(f32), jnp.zeros((4, 16), f32)], axis=1)
        blocks.append(jnp.concatenate([block, note, jnp.zeros((4, 320), f32)], axis=1))
    blank = [jnp.zeros((8, 576), f32)]
    out[8] = jnp.concatenate(rows + blank + blocks + blank, axis=0).astype(bf16)
    for one in gathered:
        one.wait()


def stash_kernel(ids, *refs):
    sources, outs, sems = refs[:4], refs[5:9], refs[9]
    here = pl.ds(pl.multiple_of(ids[0] * HALF, 128), HALF)
    copies = [pltpu.make_async_copy(sources[i].at[here], outs[i], sems.at[i]) for i in range(4)]
    for one in copies:
        one.start()
    for one in copies:
        one.wait()


def attention_kernel(ids, q, keys_mine, keys_other, *rest):
    out, told, scratch = rest[-3:]
    lane = lax.broadcasted_iota(jnp.int32, (1, 512), 1)
    start = jnp.where(lane < 256, ids[2] * 256, (ids[2] - 2 * ids[0]) * 256)
    places = (start + lane).astype(f32)
    slot = lax.broadcasted_iota(jnp.int32, (32, 128), 1)
    extra = q[8]
    notes = extra[16:32, 128:256].astype(f32)
    told[0:8, :] = extra[16:32, 0:128].astype(f32)[0:8]
    told[8:16, :] = notes[0:8]
    fresh = extra[0:16]
    row = lax.broadcasted_iota(jnp.int32, (64, 16), 0)
    col = lax.broadcasted_iota(jnp.int32, (64, 16), 1)
    keys, scores, late, weights, late_weights, top, total = ([None] * 4 for _ in range(7))
    for r in range(4):
        keys[r] = jnp.concatenate(
            [side[4 * r + j] for side in (keys_mine, keys_other) for j in range(4)], axis=0
        )
        asked = jnp.concatenate([q[r], q[4 + r]], axis=0)
        scores[r] = lax.dot_general(
            asked, keys[r], (((1,), (1,)), ((), ())), preferred_element_type=f32
        )
        late[r] = lax.dot_general(
            asked, fresh, (((1,), (1,)), ((), ())), preferred_element_type=f32
        )
    for r in range(4):
        usable = places < notes[0:1, 64 + r : 65 + r] * 128.0 + notes[0:1, 68 + r : 69 + r]
        counted = (ids[3] == 0) & ((col == r) | ((col == 4 + r) & (row >= 32)))
        scaled = jnp.where(usable, scores[r] * SCORE_SCALE, MASK_VALUE)
        late_scaled = jnp.where(counted, late[r] * SCORE_SCALE, MASK_VALUE)
        top[r] = jnp.maximum(
            jnp.max(scaled, axis=1, keepdims=True), jnp.max(late_scaled, axis=1, keepdims=True)
        )
        weights[r] = jnp.where(usable, jnp.exp(scaled - top[r]), 0.0)
        late_weights[r] = jnp.where(counted, jnp.exp(late_scaled - top[r]), 0.0)
        total[r] = jnp.sum(weights[r], axis=1, keepdims=True)
        total[r] = total[r] + jnp.sum(late_weights[r], axis=1, keepdims=True)
    for r in range(4):
        summed = jnp.dot(weights[r].astype(bf16), keys[r][:, :512], preferred_element_type=f32)
        summed = summed + jnp.dot(
            late_weights[r].astype(bf16), fresh[:, :512], preferred_element_type=f32
        )
        live = total[r] > 0.0
        safe = jnp.where(live, total[r], 1.0)
        level = jnp.where(live, top[r] + jnp.log(safe), MASK_VALUE)
        value = summed * (1.0 / safe)
        first, second, third = split(level)
        for s in range(2):
            rows = slice(32 * s, 32 * s + 32)
            tail = jnp.where(
                slot == 0,
                first[rows],
                jnp.where(slot == 1, second[rows], jnp.where(slot == 2, third[rows], 0.0)),
            )
            for k in range(5):
                part = value[rows, 128 * k : 128 * k + 128] if k < 4 else tail
                scratch[k, pl.ds(4 * s + r, 32, stride=8), :] = part
    for k in range(5):
        out[:, :, 128 * k : 128 * k + 128] = scratch[k].reshape(32, 8, 128).astype(bf16)


def context_kernel(ids, got, told, value_up, proj, kept, sent):
    level = jnp.sum(got[:, :, 512:640].astype(f32), axis=2, keepdims=True)
    factors = jnp.exp(level - jnp.max(level, axis=0, keepdims=True))
    denominator = jnp.sum(factors, axis=0)
    numerator = jnp.zeros((8, 512), f32)
    for i in range(32):
        numerator = numerator + factors[i] * got[i, :, 0:512].astype(f32)
    context = (numerator / denominator).astype(bf16)
    vals = jnp.dot(context, value_up[...], preferred_element_type=f32).astype(bf16)
    start = jnp.concatenate([told[0:8, :], jnp.zeros((8, HALF - 128), f32)], axis=1)
    start = pltpu.roll(start, (ids[2] % 32) * BLOCK, 1)
    for out, half in ((sent, 1 - ids[0]), (kept, ids[0])):
        lanes = pl.ds(pl.multiple_of(half * HALF, 128), HALF)
        total = jnp.dot(vals, proj[:, lanes], preferred_element_type=f32)
        total = total + jnp.where(ids[2] // 32 == half, start, 0.0)
        for k in range(CHUNKS):
            out[k] = total[:, 128 * k : 128 * k + 128].astype(out.dtype)


def join_kernel(kept, other, out):
    for k in range(CHUNKS):
        out[k] = (kept[k] + other[k].astype(f32)).astype(bf16)
    for k in range(CHUNKS, 32):
        out[k] = jnp.zeros((8, 128), bf16)


def spread_kernel(ids, got, told, out):
    total = got[0].astype(f32)
    for i in range(1, 32):
        total = total + got[i].astype(f32)
    piece = jnp.where(ids[3] == CHUNKS, told[8:16, :], total).astype(bf16)
    for i in range(64):
        out[i] = piece


def raise_kernel(ids, rows, gain, gate, up, gate_other, up_other, out, scaled, own):
    squares = [jnp.zeros((8, 128), f32) for _ in range(2)]
    for k in range(CHUNKS):
        lanes = slice(128 * k, 128 * k + 128)
        parts = [rows[32 * d + k].astype(f32) for d in range(2)]
        squares = [squares[d] + parts[d] * parts[d] for d in range(2)]
        both = jnp.concatenate(parts, axis=0) * gain[pl.ds(ids[0] * CHUNKS + k, 1), :]
        scaled[:, lanes] = both.astype(bf16)
        own[:, lanes] = jnp.where(ids[4] == 0, parts[0], parts[1])
    asked = scaled[...]
    out[:, 0:128] = jnp.dot(asked, gate[...], preferred_element_type=f32)
    out[:, 128:256] = jnp.dot(asked, up[...], preferred_element_type=f32)
    out[:, 256:384] = jnp.dot(asked, gate_other[...], preferred_element_type=f32)
    out[:, 384:512] = jnp.dot(asked, up_other[...], preferred_element_type=f32)
    out[:, 512:640] = jnp.concatenate(squares, axis=0)
    shift = HALF - (ids[3] % 16) * (2 * BLOCK)
    turned = pltpu.roll(own[...], shift, 1)[:, 0:256]
    out[0:8, 640:896] = jnp.where(ids[0] == ids[3] // 16, turned, 0.0)
    out[8:16, 640:896] = jnp.zeros((8, 256), f32)


def lower_kernel(ids, mine, other, rows, down, down_other, out, own, product):
    squares = jnp.sum(mine[:, 512:640] + other[:, 512:640], axis=1, keepdims=True)
    scale = lax.rsqrt(squares * (1.0 / (2 * HALF)) + EPSILON)

    def active(near, near_at, far, far_at):
        gate = (near[:, near_at : near_at + 128] + far[:, far_at : far_at + 128]) * scale
        up = (
            near[:, near_at + 128 : near_at + 256] + far[:, far_at + 128 : far_at + 256]
        ) * scale
        return (gate / (1.0 + jnp.exp(-gate)) * up).astype(bf16)

    told = jnp.concatenate([rows[CHUNKS].astype(f32), rows[32 + CHUNKS].astype(f32)], axis=0)
    lane = lax.broadcasted_iota(jnp.int32, (16, 128), 1)
    wanted = (lane % 16 == ids[4] * 8 + ids[3] // 4) & (lane < 48)
    mixing = jnp.sum(jnp.where(wanted, told, 0.0), axis=1, keepdims=True)
    here = active(mine, 0, other, 256)
    there = active(other, 0, mine, 256)
    for k in range(14):
        lanes = slice(512 * k, 512 * k + 512)
        total = jnp.dot(here, down[:, lanes], preferred_element_type=f32)
        total = total + jnp.dot(there, down_other[:, lanes], preferred_element_type=f32)
        product[:, lanes] = total * mixing
    product[:, 7168:7296] = jnp.zeros((16, 128), f32)
    both = mine[0:8, 640:896] + other[0:8, 640:896]

    def fill(core):
        for k in range(32):
            at = (2 * k + core) * BLOCK
            base, turn = at // 128 * 128, at % 128
            for d in range(2):
                part = product[8 * d : 8 * d + 8, base : base + 256]
                if turn:
                    part = pltpu.roll(part, 256 - turn, 1)
                out[32 * d + k] = part[:, 0:128].astype(bf16)
        part = pltpu.roll(both, 256 - BLOCK, 1) if core else both
        own[...] = part[:, 0:128]

    @pl.when(ids[0] == 0)
    def _():
        fill(0)

    @pl.when(ids[0] == 1)
    def _():
        fill(1)


def finish_kernel(got, own, out):
    total = own[...]
    for i in range(64):
        total = total + got[i].astype(f32)
    for s in range(2):
        out[s] = total[4 * s : 4 * s + 4, 0:BLOCK].astype(bf16)


def body(
    prompt_pool,
    block_table,
    cache_len,
    queries,
    fresh_latent,
    x_in,
    routes,
    gates,
    norm_gain,
    value_up,
    out_proj,
    w_gate,
    w_up,
    w_down,
):
    role = lax.axis_index("role")
    dp = lax.axis_index("dp")
    core = lax.axis_index("core")
    chip = lax.axis_index("x") * lax.axis_size("z") + lax.axis_index("z")
    ids = jnp.stack([core, 1 - role, chip * 2 + core, chip, dp]).astype(jnp.int32)
    half_there = (1 - core) * HALF
    gate_other, up_other, down_other = [
        swap(one, "core") for one in (w_gate[0], w_up[0], w_down[0])
    ]
    given = (
        queries.reshape(8, 64, 576),
        fresh_latent.reshape(2, 4, 576),
        x_in.reshape(2, 4, BLOCK),
        routes.reshape(2, 4, 8),
        gates.reshape(2, 4, 8),
        cache_len.reshape(1, 4),
        block_table[:, 0, 0],
    )
    picked, keys = call(
        pick_kernel,
        [shape(9, 32, 576), shape(16, 64, 576)],
        [SM] + [FAR] * 8,
        (ids,) + tuple(far(one) for one in given + (prompt_pool[0, 0, 0],)),
        19000000,
        900000,
        [pltpu.VMEM(one.shape, one.dtype) for one in given[:6]]
        + [pltpu.SMEM((2, 4, 4), jnp.int32), pltpu.VMEM((5, 512, 128), f32)]
        + [pltpu.SemaphoreType.DMA((26,))],
        8,
    )
    q = swap(picked, "role")
    keys_other = swap(keys, "core")
    halves = pl.pallas_call(
        stash_kernel,
        out_shape=[pltpu.VMEM((HALF, 128), bf16)] * 4,
        in_specs=[SM] + [FAR] * 4 + [ANY],
        out_specs=[VM] * 4,
        scratch_shapes=[pltpu.SemaphoreType.DMA((4,))],
        compiler_params=pltpu.CompilerParams(vmem_limit_bytes=4 * MIB),
        cost_estimate=pl.CostEstimate(flops=0, bytes_accessed=7400000, transcendentals=0),
    )(ids, *[far(one) for one in (w_gate[0], w_up[0], gate_other, up_other)], picked)
    after = (*halves, down_other)[:EXTRA]
    sent, told = call(
        attention_kernel,
        [shape(32, 8, 640), shape(16, 128, dtype=f32)],
        [SM, VM, VM, VM] + [ANY] * len(after),
        (ids, q, keys, keys_other) + after,
        300000000,
        4000000,
        [pltpu.VMEM((5, 256, 128), f32)],
        16,
        131072,
    )
    got = exchange(sent, XZ)
    kept, passed = call(
        context_kernel,
        [shape(CHUNKS, 8, 128, dtype=f32), shape(CHUNKS, 8, 128)],
        [SM] + [VM] * 4,
        (ids, got, told, value_up[0], out_proj),
        20000000,
        2500000,
        (),
        8,
    )
    partial = call(
        join_kernel, shape(32, 8, 128), [VM] * 2, (kept, swap(passed, "core")), 30000, 200000, (), 4
    )
    rows = exchange(
        call(
            spread_kernel,
            shape(64, 8, 128),
            [SM, VM, VM],
            (ids, exchange(partial, XZ), told),
            40000,
            200000,
            (),
            4,
        ),
        DXZ,
    )
    raised = call(
        raise_kernel,
        shape(16, 896, dtype=f32),
        [SM] + [VM] * 6,
        (ids, rows, norm_gain.reshape(56, 128), *halves),
        60000000,
        6000000,
        [pltpu.VMEM((16, HALF), bf16), pltpu.VMEM((8, HALF), f32)],
        16,
    )
    raised_other = swap(raised, "core")
    outgoing, own = call(
        lower_kernel,
        [shape(64, 8, 128), shape(8, 128, dtype=f32)],
        [SM] + [VM] * 5,
        (ids, raised, raised_other, rows, w_down[0], down_other),
        60000000,
        4000000,
        [pltpu.VMEM((16, 7296), f32)],
        16,
        4096,
    )
    done = call(
        finish_kernel, shape(2, 4, BLOCK), [VM] * 2, (exchange(outgoing, DXZ), own), 70000, 140000, (), 4
    )
    return swap(done, "role").reshape(2, 1, 1, 4, BLOCK)


EXTRA = 6


def solution(mesh):
    split = Mesh(mesh.devices.reshape(2, 2, 4, 8, 2), ("role", "dp", "x", "z", "core"))
    e = ("x", "z", "core")
    slab = ("dp", "x", "z", "core")
    placed = (
        P("role", "dp", e, None, None, None),
        P(None, "dp", e, None, None),
        P("role", "dp", None),
        P(None, "role", "dp", None, None, None),
        P(None, "role", "dp", None, None),
        P(None, "role", "dp", None, e),
        P(None, "role", "dp", None, None),
        P(None, "role", "dp", None, None),
        P(),
        P(e, None, None),
        P(e, None),
        P(slab, None, None),
        P(slab, None, None),
        P(slab, None, None),
    )
    return jax.shard_map(
        body,
        mesh=split,
        in_specs=placed,
        out_specs=P(None, "role", "dp", None, e),
        check_vma=False,
    )
```

```python
import jax
import jax.numpy as jnp
from jax import lax
from jax.experimental import pallas as pl
from jax.experimental.pallas import tpu as pltpu
from jax.sharding import Mesh, PartitionSpec as P

SCORE_SCALE = 192.0 ** (-0.5)
EPSILON = 1e-06
MASK_VALUE = -1e30
HALF = 3584
CHUNKS = 28
BLOCK = 112
XZ = ("x", "z")
DXZ = ("dp", "x", "z")
bf16 = jnp.bfloat16
f32 = jnp.float32

VM = pl.BlockSpec(memory_space=pltpu.VMEM)
SM = pl.BlockSpec(memory_space=pltpu.SMEM)
ANY = pl.BlockSpec(memory_space=pl.ANY)
FAR = pl.BlockSpec(memory_space=pltpu.HBM)
MIB = 1024 * 1024


def call(kernel, outs, specs, args, flops, moved, scratch=(), limit=16, exps=0):
    many = isinstance(outs, list)
    return pl.pallas_call(
        kernel,
        out_shape=outs,
        in_specs=specs,
        out_specs=[VM] * len(outs) if many else VM,
        scratch_shapes=list(scratch),
        compiler_params=pltpu.CompilerParams(vmem_limit_bytes=limit * MIB),
        cost_estimate=pl.CostEstimate(flops=flops, bytes_accessed=moved, transcendentals=exps),
    )(*args)


def shape(*dims, dtype=bf16):
    return jax.ShapeDtypeStruct(dims, dtype)


def far(value):
    return pltpu.with_memory_space_constraint(value, pltpu.HBM)


def swap(value, axis):
    return lax.ppermute(value, axis, [(0, 1), (1, 0)])


def exchange(value, axes):
    return lax.all_to_all(value, axes, 0, 0, tiled=True)


def split(value):
    first = value.astype(bf16).astype(f32)
    second = (value - first).astype(bf16).astype(f32)
    return first, second, (value - first) - second


def pick_kernel(ids, *refs):
    sources, pool, (out, keys), landed, (wide, sems) = refs[:7], refs[7], refs[8:10], refs[10:17], refs[17:]
    copies = [
        pltpu.make_async_copy(
            sources[0].at[pl.ds(2 * i, 2)], landed[0].at[pl.ds(2 * i, 2)], sems.at[i]
        )
        for i in range(4)
    ] + [pltpu.make_async_copy(sources[i], landed[i], sems.at[3 + i]) for i in range(1, 7)]
    copies[9].start()
    for one in copies[:9]:
        one.start()
    queries, fresh, x_in, routes, gates, lengths, table = landed
    copies[9].wait()
    gathered = [
        pltpu.make_async_copy(
            pool.at[table[ids[1], i // 4, i % 4]], keys.at[i], sems.at[10 + i]
        )
        for i in range(16)
    ]
    for one in gathered:
        one.start()
    for i in range(8):
        if i % 2 == 0:
            copies[i // 2].wait()
        asked = queries[i].astype(f32)
        for k in range(5):
            lanes = slice(128 * k, min(128 * k + 128, 576))
            wide[k, 64 * i : 64 * i + 64, 0 : lanes.stop - lanes.start] = asked[:, lanes]
        for k in range(5):
            lanes = slice(128 * k, min(128 * k + 128, 576))
            half = wide[k, pl.ds(64 * i + ids[0], 32, stride=2), :]
            half = half[:, 0 : lanes.stop - lanes.start].astype(bf16)
            out[2 * i, :, lanes] = half[0:16]
            out[2 * i + 1, :, lanes] = half[16:32]
    lane = lax.broadcasted_iota(jnp.int32, (4, 128), 1)
    for one in copies[4:9]:
        one.wait()
    count = jnp.concatenate([lengths[...], jnp.zeros((1, 124), jnp.int32)], axis=1)
    high = lax.shift_right_logical(count, 7)
    told = pltpu.roll(high.astype(f32), 64, 1) + pltpu.roll((count - 128 * high).astype(f32), 68, 1)
    rows = []
    blocks = []
    for s in range(2):
        note = jnp.zeros((4, 128), f32)
        for k in range(8):
            note = note + jnp.where(lane == routes[s][:, k : k + 1], gates[s][:, k : k + 1], 0.0)
        parts = split(note)
        note = parts[0] + pltpu.roll(parts[1], 16, 1) + pltpu.roll(parts[2], 32, 1) + told
        rows.append(fresh[s].astype(f32))
        block = jnp.concatenate([x_in[s].astype(f32), jnp.zeros((4, 16), f32)], axis=1)
        blocks.append(jnp.concatenate([block, note, jnp.zeros((4, 320), f32)], axis=1))
    out[16] = jnp.concatenate(rows + blocks, axis=0).astype(bf16)
    for one in gathered:
        one.wait()


def stash_kernel(ids, *refs):
    sources, (raising, sems) = refs[:4], refs[5:]
    here = pl.ds(pl.multiple_of(ids[0] * HALF, 128), HALF)
    copies = [
        pltpu.make_async_copy(
            sources[i].at[here], raising.at[:, pl.ds(128 * i, 128)], sems.at[i]
        )
        for i in range(4)
    ]
    for one in copies:
        one.start()
    for one in copies:
        one.wait()


def attention_kernel(ids, q, keys_mine, keys_other, *rest):
    out, told, scratch = rest[-3:]
    lane = lax.broadcasted_iota(jnp.int32, (1, 512), 1)
    start = jnp.where(lane < 256, ids[2] * 256, (ids[2] - 2 * ids[0]) * 256)
    places = (start + lane).astype(f32)
    slot = lax.broadcasted_iota(jnp.int32, (32, 128), 1)
    fresh = q[16]
    notes = fresh[:, 0:256].astype(f32)
    told[0:8, :] = notes[8:16, 0:128]
    told[8:16, :] = notes[8:16, 128:256]
    notes = notes[8:9, 128:256]
    row = lax.broadcasted_iota(jnp.int32, (64, 16), 0)
    col = lax.broadcasted_iota(jnp.int32, (64, 16), 1)
    keys, scores, late, weights, late_weights, top, total = ([None] * 4 for _ in range(7))
    for r in range(4):
        keys[r] = jnp.concatenate(
            [side[4 * r + j] for side in (keys_mine, keys_other) for j in range(4)], axis=0
        )
        asked = jnp.concatenate([q[2 * r], q[2 * r + 1], q[2 * r + 8], q[2 * r + 9]], axis=0)
        scores[r] = lax.dot_general(
            asked, keys[r], (((1,), (1,)), ((), ())), preferred_element_type=f32
        )
        late[r] = lax.dot_general(
            asked, fresh, (((1,), (1,)), ((), ())), preferred_element_type=f32
        )
    for r in range(4):
        usable = places < notes[0:1, 64 + r : 65 + r] * 128.0 + notes[0:1, 68 + r : 69 + r]
        counted = (ids[3] == 0) & ((col == r) | ((col == 4 + r) & (row >= 32)))
        scaled = jnp.where(usable, scores[r] * SCORE_SCALE, MASK_VALUE)
        late_scaled = jnp.where(counted, late[r] * SCORE_SCALE, MASK_VALUE)
        top[r] = jnp.maximum(
            jnp.max(scaled, axis=1, keepdims=True), jnp.max(late_scaled, axis=1, keepdims=True)
        )
        weights[r] = jnp.where(usable, jnp.exp(scaled - top[r]), 0.0)
        late_weights[r] = jnp.where(counted, jnp.exp(late_scaled - top[r]), 0.0)
        total[r] = jnp.sum(weights[r], axis=1, keepdims=True)
        total[r] = total[r] + jnp.sum(late_weights[r], axis=1, keepdims=True)
    for r in range(4):
        summed = jnp.dot(weights[r].astype(bf16), keys[r][:, :512], preferred_element_type=f32)
        summed = summed + jnp.dot(
            late_weights[r].astype(bf16), fresh[:, :512], preferred_element_type=f32
        )
        live = total[r] > 0.0
        safe = jnp.where(live, total[r], 1.0)
        level = jnp.where(live, top[r] + jnp.log(safe), MASK_VALUE)
        value = summed * (1.0 / safe)
        first, second, third = split(level)
        for s in range(2):
            rows = slice(32 * s, 32 * s + 32)
            tail = jnp.where(
                slot == 0,
                first[rows],
                jnp.where(slot == 1, second[rows], jnp.where(slot == 2, third[rows], 0.0)),
            )
            for k in range(5):
                part = value[rows, 128 * k : 128 * k + 128] if k < 4 else tail
                scratch[k, pl.ds(4 * s + r, 32, stride=8), :] = part
    for k in range(5):
        out[:, :, 128 * k : 128 * k + 128] = scratch[k].reshape(32, 8, 128).astype(bf16)


def project(ids, half, vals, told, proj, out):
    lanes = pl.ds(pl.multiple_of(half * HALF, 128), HALF)
    total = jnp.dot(vals[...], proj[:, lanes], preferred_element_type=f32)
    start = jnp.concatenate([told[0:8, :], jnp.zeros((8, HALF - 128), f32)], axis=1)
    start = pltpu.roll(start, (ids[2] % 32) * BLOCK, 1)
    total = total + jnp.where(ids[2] // 32 == half, start, 0.0)
    for k in range(CHUNKS):
        out[k] = total[:, 128 * k : 128 * k + 128].astype(out.dtype)


def context_kernel(ids, got, told, value_up, proj, vals, sent):
    level = jnp.sum(got[:, :, 512:640].astype(f32), axis=2, keepdims=True)
    factors = jnp.exp(level - jnp.max(level, axis=0, keepdims=True))
    denominator = jnp.sum(factors, axis=0)
    numerator = jnp.zeros((8, 512), f32)
    for i in range(32):
        numerator = numerator + factors[i] * got[i, :, 0:512].astype(f32)
    context = (numerator / denominator).astype(bf16)
    vals[...] = jnp.dot(context, value_up[...], preferred_element_type=f32).astype(bf16)
    project(ids, 1 - ids[0], vals, told, proj, sent)


def kept_kernel(ids, vals, told, proj, kept):
    project(ids, ids[0], vals, told, proj, kept)


def join_kernel(kept, other, out):
    for k in range(CHUNKS):
        out[k] = (kept[k] + other[k].astype(f32)).astype(bf16)
    for k in range(CHUNKS, 32):
        out[k] = jnp.zeros((8, 128), bf16)


def spread_kernel(ids, got, told, out):
    total = got[0].astype(f32)
    for i in range(1, 32):
        total = total + got[i].astype(f32)
    piece = jnp.where(ids[3] == CHUNKS, told[8:16, :], total).astype(bf16)
    for i in range(64):
        out[i] = piece


def raise_kernel(ids, rows, gain, weights, out, scaled, own):
    squares = [jnp.zeros((8, 128), f32) for _ in range(2)]
    for k in range(CHUNKS):
        lanes = slice(128 * k, 128 * k + 128)
        parts = [rows[32 * d + k].astype(f32) for d in range(2)]
        squares = [squares[d] + parts[d] * parts[d] for d in range(2)]
        both = jnp.concatenate(parts, axis=0) * gain[pl.ds(ids[0] * CHUNKS + k, 1), :]
        scaled[:, lanes] = both.astype(bf16)
        own[:, lanes] = jnp.where(ids[4] == 0, parts[0], parts[1])
    out[:, 0:512] = jnp.dot(scaled[...], weights[...], preferred_element_type=f32)
    out[:, 512:640] = jnp.concatenate(squares, axis=0)
    shift = HALF - (ids[3] % 16) * (2 * BLOCK)
    turned = pltpu.roll(own[...], shift, 1)[:, 0:256]
    out[0:8, 640:896] = jnp.where(ids[0] == ids[3] // 16, turned, 0.0)
    out[8:16, 640:896] = jnp.zeros((8, 256), f32)


def lower_kernel(ids, mine, other, rows, down, down_other, out, own, product):
    squares = jnp.sum(mine[:, 512:640] + other[:, 512:640], axis=1, keepdims=True)
    scale = lax.rsqrt(squares * (1.0 / (2 * HALF)) + EPSILON)

    def active(near, near_at, far, far_at):
        gate = (near[:, near_at : near_at + 128] + far[:, far_at : far_at + 128]) * scale
        up = (
            near[:, near_at + 128 : near_at + 256] + far[:, far_at + 128 : far_at + 256]
        ) * scale
        return (gate / (1.0 + jnp.exp(-gate)) * up).astype(bf16)

    told = jnp.concatenate([rows[CHUNKS].astype(f32), rows[32 + CHUNKS].astype(f32)], axis=0)
    lane = lax.broadcasted_iota(jnp.int32, (16, 128), 1)
    wanted = (lane % 16 == ids[4] * 8 + ids[3] // 4) & (lane < 48)
    mixing = jnp.sum(jnp.where(wanted, told, 0.0), axis=1, keepdims=True)
    here = active(mine, 0, other, 256)
    there = active(other, 0, mine, 256)
    for k in range(14):
        lanes = slice(512 * k, 512 * k + 512)
        total = jnp.dot(here, down[:, lanes], preferred_element_type=f32)
        total = total + jnp.dot(there, down_other[:, lanes], preferred_element_type=f32)
        product[:, lanes] = total * mixing
    product[:, 7168:7296] = jnp.zeros((16, 128), f32)
    both = mine[0:8, 640:896] + other[0:8, 640:896]

    def fill(core):
        for k in range(32):
            at = (2 * k + core) * BLOCK
            base, turn = at // 128 * 128, at % 128
            for d in range(2):
                part = product[8 * d : 8 * d + 8, base : base + 256]
                if turn:
                    part = pltpu.roll(part, 256 - turn, 1)
                out[32 * d + k] = part[:, 0:128].astype(bf16)
        part = pltpu.roll(both, 256 - BLOCK, 1) if core else both
        own[...] = part[:, 0:128]

    @pl.when(ids[0] == 0)
    def _():
        fill(0)

    @pl.when(ids[0] == 1)
    def _():
        fill(1)


def finish_kernel(got, own, out):
    total = own[...]
    for i in range(64):
        total = total + got[i].astype(f32)
    for s in range(2):
        out[s] = total[4 * s : 4 * s + 4, 0:BLOCK].astype(bf16)


def body(
    prompt_pool,
    block_table,
    cache_len,
    queries,
    fresh_latent,
    x_in,
    routes,
    gates,
    norm_gain,
    value_up,
    out_proj,
    w_gate,
    w_up,
    w_down,
):
    role = lax.axis_index("role")
    dp = lax.axis_index("dp")
    core = lax.axis_index("core")
    chip = lax.axis_index("x") * lax.axis_size("z") + lax.axis_index("z")
    ids = jnp.stack([core, 1 - role, chip * 2 + core, chip, dp]).astype(jnp.int32)
    half_there = (1 - core) * HALF
    gate_other, up_other, down_other = [
        swap(one, "core") for one in (w_gate[0], w_up[0], w_down[0])
    ]
    given = (
        queries.reshape(8, 64, 576),
        fresh_latent.reshape(2, 4, 576),
        x_in.reshape(2, 4, BLOCK),
        routes.reshape(2, 4, 8),
        gates.reshape(2, 4, 8),
        cache_len.reshape(1, 4),
        block_table[:, 0, 0],
    )
    picked, keys = call(
        pick_kernel,
        [shape(17, 16, 576), shape(16, 64, 576)],
        [SM] + [FAR] * 8,
        (ids,) + tuple(far(one) for one in given + (prompt_pool[0, 0, 0],)),
        19000000,
        900000,
        [pltpu.VMEM(one.shape, one.dtype) for one in given[:6]]
        + [pltpu.SMEM((2, 4, 4), jnp.int32), pltpu.VMEM((5, 512, 128), f32)]
        + [pltpu.SemaphoreType.DMA((26,))],
        8,
    )
    q = swap(picked, "role")
    keys_other = swap(keys, "core")
    raising = pl.pallas_call(
        stash_kernel,
        out_shape=pltpu.VMEM((HALF, 512), bf16),
        in_specs=[SM] + [FAR] * 4 + [ANY],
        out_specs=VM,
        scratch_shapes=[pltpu.SemaphoreType.DMA((4,))],
        compiler_params=pltpu.CompilerParams(vmem_limit_bytes=4 * MIB),
        cost_estimate=pl.CostEstimate(flops=0, bytes_accessed=7400000, transcendentals=0),
    )(
        ids,
        *[far(one) for one in (w_gate[0], w_up[0], gate_other, up_other)],
        picked,
    )
    after = (raising, down_other)
    sent, told = call(
        attention_kernel,
        [shape(32, 8, 640), shape(16, 128, dtype=f32)],
        [SM, VM, VM, VM] + [ANY] * len(after),
        (ids, q, keys, keys_other) + after,
        300000000,
        4000000,
        [pltpu.VMEM((5, 256, 128), f32)],
        16,
        131072,
    )
    got = exchange(sent, XZ)
    vals, passed = call(
        context_kernel,
        [shape(8, 128), shape(CHUNKS, 8, 128)],
        [SM] + [VM] * 4,
        (ids, got, told, value_up[0], out_proj),
        12000000,
        1500000,
        (),
        8,
    )
    kept = call(
        kept_kernel,
        shape(CHUNKS, 8, 128, dtype=f32),
        [SM] + [VM] * 3,
        (ids, vals, told, out_proj),
        8000000,
        1000000,
        (),
        8,
    )
    partial = call(
        join_kernel, shape(32, 8, 128), [VM] * 2, (kept, swap(passed, "core")), 30000, 200000, (), 4
    )
    rows = exchange(
        call(
            spread_kernel,
            shape(64, 8, 128),
            [SM, VM, VM],
            (ids, exchange(partial, XZ), told),
            40000,
            200000,
            (),
            4,
        ),
        DXZ,
    )
    raised = call(
        raise_kernel,
        shape(16, 896, dtype=f32),
        [SM] + [VM] * 3,
        (ids, rows, norm_gain.reshape(56, 128), raising),
        60000000,
        6000000,
        [pltpu.VMEM((16, HALF), bf16), pltpu.VMEM((8, HALF), f32)],
        16,
    )
    raised_other = swap(raised, "core")
    outgoing, own = call(
        lower_kernel,
        [shape(64, 8, 128), shape(8, 128, dtype=f32)],
        [SM] + [VM] * 5,
        (ids, raised, raised_other, rows, w_down[0], down_other),
        60000000,
        4000000,
        [pltpu.VMEM((16, 7296), f32)],
        16,
        4096,
    )
    done = call(
        finish_kernel, shape(2, 4, BLOCK), [VM] * 2, (exchange(outgoing, DXZ), own), 70000, 140000, (), 4
    )
    return swap(done, "role").reshape(2, 1, 1, 4, BLOCK)


def solution(mesh):
    split = Mesh(mesh.devices.reshape(2, 2, 4, 8, 2), ("role", "dp", "x", "z", "core"))
    e = ("x", "z", "core")
    slab = ("dp", "x", "z", "core")
    placed = (
        P("role", "dp", e, None, None, None),
        P(None, "dp", e, None, None),
        P("role", "dp", None),
        P(None, "role", "dp", None, None, None),
        P(None, "role", "dp", None, None),
        P(None, "role", "dp", None, e),
        P(None, "role", "dp", None, None),
        P(None, "role", "dp", None, None),
        P(),
        P(e, None, None),
        P(e, None),
        P(slab, None, None),
        P(slab, None, None),
        P(slab, None, None),
    )
    return jax.shard_map(
        body,
        mesh=split,
        in_specs=placed,
        out_specs=P(None, "role", "dp", None, e),
        check_vma=False,
    )
```

```python
import jax
import jax.numpy as jnp
from jax import lax
from jax.experimental import pallas as pl
from jax.experimental.pallas import tpu as pltpu
from jax.sharding import Mesh, PartitionSpec as P

SCORE_SCALE = 192.0 ** (-0.5)
EPSILON = 1e-06
MASK_VALUE = -1e30
HALF = 3584
CHUNKS = 28
BLOCK = 112
XZ = ("x", "z")
DXZ = ("dp", "x", "z")
bf16 = jnp.bfloat16
f32 = jnp.float32

VM = pl.BlockSpec(memory_space=pltpu.VMEM)
ANY = pl.BlockSpec(memory_space=pl.ANY)
FAR = pl.BlockSpec(memory_space=pltpu.HBM)
MIB = 1024 * 1024


def call(kernel, outs, specs, args, flops, moved, scratch=(), limit=16, exps=0):
    many = isinstance(outs, list)
    return pl.pallas_call(
        kernel,
        out_shape=outs,
        in_specs=specs,
        out_specs=[VM] * len(outs) if many else VM,
        scratch_shapes=list(scratch),
        compiler_params=pltpu.CompilerParams(vmem_limit_bytes=limit * MIB),
        cost_estimate=pl.CostEstimate(flops=flops, bytes_accessed=moved, transcendentals=exps),
    )(*args)


def shape(*dims, dtype=bf16):
    return jax.ShapeDtypeStruct(dims, dtype)


def far(value):
    return pltpu.with_memory_space_constraint(value, pltpu.HBM)


def swap(value, axis):
    return lax.ppermute(value, axis, [(0, 1), (1, 0)])


def exchange(value, axes):
    return lax.all_to_all(value, axes, 0, 0, tiled=True)


def spot():
    core = lax.axis_index("core")
    chip = lax.axis_index("x") * 8 + lax.axis_index("z")
    return core, 1 - lax.axis_index("role"), chip * 2 + core, chip, lax.axis_index("dp")


def split(value):
    first = value.astype(bf16).astype(f32)
    second = (value - first).astype(bf16).astype(f32)
    return first, second, (value - first) - second


def pick_kernel(*refs):
    ids = spot()
    sources, pool, (out, keys), landed, (wide, sems) = refs[:7], refs[7], refs[8:10], refs[10:17], refs[17:]
    copies = [
        pltpu.make_async_copy(
            sources[0].at[pl.ds(2 * i, 2)], landed[0].at[pl.ds(2 * i, 2)], sems.at[i]
        )
        for i in range(4)
    ] + [pltpu.make_async_copy(sources[i], landed[i], sems.at[3 + i]) for i in range(1, 7)]
    copies[9].start()
    for one in copies[:9]:
        one.start()
    queries, fresh, x_in, routes, gates, lengths, table = landed
    copies[9].wait()
    gathered = [
        pltpu.make_async_copy(
            pool.at[table[ids[1], i // 4, i % 4]], keys.at[i], sems.at[10 + i]
        )
        for i in range(16)
    ]
    for one in gathered:
        one.start()
    for i in range(8):
        if i % 2 == 0:
            copies[i // 2].wait()
        asked = queries[i].astype(f32)
        for k in range(5):
            lanes = slice(128 * k, min(128 * k + 128, 576))
            wide[k, 64 * i : 64 * i + 64, 0 : lanes.stop - lanes.start] = asked[:, lanes]
        for k in range(5):
            lanes = slice(128 * k, min(128 * k + 128, 576))
            half = wide[k, pl.ds(64 * i + ids[0], 32, stride=2), :]
            half = half[:, 0 : lanes.stop - lanes.start].astype(bf16)
            out[2 * i, :, lanes] = half[0:16]
            out[2 * i + 1, :, lanes] = half[16:32]
    lane = lax.broadcasted_iota(jnp.int32, (4, 128), 1)
    for one in copies[4:9]:
        one.wait()
    count = jnp.concatenate([lengths[...], jnp.zeros((1, 124), jnp.int32)], axis=1)
    high = lax.shift_right_logical(count, 7)
    told = pltpu.roll(high.astype(f32), 64, 1) + pltpu.roll((count - 128 * high).astype(f32), 68, 1)
    rows = []
    blocks = []
    for s in range(2):
        note = jnp.zeros((4, 128), f32)
        for k in range(8):
            note = note + jnp.where(lane == routes[s][:, k : k + 1], gates[s][:, k : k + 1], 0.0)
        parts = split(note)
        note = parts[0] + pltpu.roll(parts[1], 16, 1) + pltpu.roll(parts[2], 32, 1) + told
        rows.append(fresh[s].astype(f32))
        block = jnp.concatenate([x_in[s].astype(f32), jnp.zeros((4, 16), f32)], axis=1)
        blocks.append(jnp.concatenate([block, note, jnp.zeros((4, 320), f32)], axis=1))
    out[16] = jnp.concatenate(rows + blocks, axis=0).astype(bf16)
    for one in gathered:
        one.wait()


def stash_kernel(*refs):
    ids = spot()
    sources, (raising, sems) = refs[:4], refs[5:]
    here = pl.ds(pl.multiple_of(ids[0] * HALF, 128), HALF)
    copies = [
        pltpu.make_async_copy(
            sources[i].at[here], raising.at[:, pl.ds(128 * i, 128)], sems.at[i]
        )
        for i in range(4)
    ]
    for one in copies:
        one.start()
    for one in copies:
        one.wait()


def attention_kernel(q, keys_mine, keys_other, *rest):
    ids = spot()
    out, told, scratch = rest[-3:]
    lane = lax.broadcasted_iota(jnp.int32, (1, 512), 1)
    start = jnp.where(lane < 256, ids[2] * 256, (ids[2] - 2 * ids[0]) * 256)
    places = (start + lane).astype(f32)
    slot = lax.broadcasted_iota(jnp.int32, (32, 128), 1)
    fresh = q[16]
    notes = fresh[:, 0:256].astype(f32)
    told[0:8, :] = notes[8:16, 0:128]
    told[8:16, :] = notes[8:16, 128:256]
    notes = notes[8:9, 128:256]
    row = lax.broadcasted_iota(jnp.int32, (64, 16), 0)
    col = lax.broadcasted_iota(jnp.int32, (64, 16), 1)
    keys, scores, late, weights, late_weights, top, total = ([None] * 4 for _ in range(7))
    for r in range(4):
        keys[r] = jnp.concatenate(
            [side[4 * r + j] for side in (keys_mine, keys_other) for j in range(4)], axis=0
        )
        asked = jnp.concatenate([q[2 * r], q[2 * r + 1], q[2 * r + 8], q[2 * r + 9]], axis=0)
        scores[r] = lax.dot_general(
            asked, keys[r], (((1,), (1,)), ((), ())), preferred_element_type=f32
        )
        late[r] = lax.dot_general(
            asked, fresh, (((1,), (1,)), ((), ())), preferred_element_type=f32
        )
    for r in range(4):
        usable = places < notes[0:1, 64 + r : 65 + r] * 128.0 + notes[0:1, 68 + r : 69 + r]
        counted = (ids[3] == 0) & ((col == r) | ((col == 4 + r) & (row >= 32)))
        scaled = jnp.where(usable, scores[r] * SCORE_SCALE, MASK_VALUE)
        late_scaled = jnp.where(counted, late[r] * SCORE_SCALE, MASK_VALUE)
        top[r] = jnp.maximum(
            jnp.max(scaled, axis=1, keepdims=True), jnp.max(late_scaled, axis=1, keepdims=True)
        )
        weights[r] = jnp.where(usable, jnp.exp(scaled - top[r]), 0.0)
        late_weights[r] = jnp.where(counted, jnp.exp(late_scaled - top[r]), 0.0)
        total[r] = jnp.sum(weights[r], axis=1, keepdims=True)
        total[r] = total[r] + jnp.sum(late_weights[r], axis=1, keepdims=True)
    for r in range(4):
        summed = jnp.dot(weights[r].astype(bf16), keys[r][:, :512], preferred_element_type=f32)
        summed = summed + jnp.dot(
            late_weights[r].astype(bf16), fresh[:, :512], preferred_element_type=f32
        )
        live = total[r] > 0.0
        safe = jnp.where(live, total[r], 1.0)
        level = jnp.where(live, top[r] + jnp.log(safe), MASK_VALUE)
        value = summed * (1.0 / safe)
        first, second, third = split(level)
        for s in range(2):
            rows = slice(32 * s, 32 * s + 32)
            tail = jnp.where(
                slot == 0,
                first[rows],
                jnp.where(slot == 1, second[rows], jnp.where(slot == 2, third[rows], 0.0)),
            )
            for k in range(5):
                part = value[rows, 128 * k : 128 * k + 128] if k < 4 else tail
                scratch[k, pl.ds(4 * s + r, 32, stride=8), :] = part
    for k in range(5):
        out[:, :, 128 * k : 128 * k + 128] = scratch[k].reshape(32, 8, 128).astype(bf16)


def project(ids, half, vals, told, proj, out):
    lanes = pl.ds(pl.multiple_of(half * HALF, 128), HALF)
    total = jnp.dot(vals[...], proj[:, lanes], preferred_element_type=f32)
    start = jnp.concatenate([told[0:8, :], jnp.zeros((8, HALF - 128), f32)], axis=1)
    start = pltpu.roll(start, (ids[2] % 32) * BLOCK, 1)
    total = total + jnp.where(ids[2] // 32 == half, start, 0.0)
    for k in range(CHUNKS):
        out[k] = total[:, 128 * k : 128 * k + 128].astype(out.dtype)


def context_kernel(got, told, value_up, proj, vals, sent):
    ids = spot()
    level = jnp.sum(got[:, :, 512:640].astype(f32), axis=2, keepdims=True)
    factors = jnp.exp(level - jnp.max(level, axis=0, keepdims=True))
    denominator = jnp.sum(factors, axis=0)
    numerator = jnp.zeros((8, 512), f32)
    for i in range(32):
        numerator = numerator + factors[i] * got[i, :, 0:512].astype(f32)
    context = (numerator / denominator).astype(bf16)
    vals[...] = jnp.dot(context, value_up[...], preferred_element_type=f32).astype(bf16)
    project(ids, 1 - ids[0], vals, told, proj, sent)


def kept_kernel(vals, told, proj, kept):
    ids = spot()
    project(ids, ids[0], vals, told, proj, kept)


def join_kernel(kept, other, out):
    for k in range(CHUNKS):
        out[k] = (kept[k] + other[k].astype(f32)).astype(bf16)
    for k in range(CHUNKS, 32):
        out[k] = jnp.zeros((8, 128), bf16)


def spread_kernel(got, told, out):
    ids = spot()
    total = got[0].astype(f32)
    for i in range(1, 32):
        total = total + got[i].astype(f32)
    piece = jnp.where(ids[3] == CHUNKS, told[8:16, :], total).astype(bf16)
    for i in range(64):
        out[i] = piece


def raise_kernel(rows, gain, weights, out, scaled, own):
    ids = spot()
    squares = [jnp.zeros((8, 128), f32) for _ in range(2)]
    for k in range(CHUNKS):
        lanes = slice(128 * k, 128 * k + 128)
        parts = [rows[32 * d + k].astype(f32) for d in range(2)]
        squares = [squares[d] + parts[d] * parts[d] for d in range(2)]
        both = jnp.concatenate(parts, axis=0) * gain[pl.ds(ids[0] * CHUNKS + k, 1), :]
        scaled[:, lanes] = both.astype(bf16)
        own[:, lanes] = jnp.where(ids[4] == 0, parts[0], parts[1])
    out[:, 0:512] = jnp.dot(scaled[...], weights[...], preferred_element_type=f32)
    out[:, 512:640] = jnp.concatenate(squares, axis=0)
    shift = HALF - (ids[3] % 16) * (2 * BLOCK)
    turned = pltpu.roll(own[...], shift, 1)[:, 0:256]
    out[0:8, 640:896] = jnp.where(ids[0] == ids[3] // 16, turned, 0.0)
    out[8:16, 640:896] = jnp.zeros((8, 256), f32)


def lower_kernel(mine, other, rows, down, down_other, out, own, product):
    ids = spot()
    squares = jnp.sum(mine[:, 512:640] + other[:, 512:640], axis=1, keepdims=True)
    scale = lax.rsqrt(squares * (1.0 / (2 * HALF)) + EPSILON)

    def active(near, near_at, far, far_at):
        gate = (near[:, near_at : near_at + 128] + far[:, far_at : far_at + 128]) * scale
        up = (
            near[:, near_at + 128 : near_at + 256] + far[:, far_at + 128 : far_at + 256]
        ) * scale
        return (gate / (1.0 + jnp.exp(-gate)) * up).astype(bf16)

    told = jnp.concatenate([rows[CHUNKS].astype(f32), rows[32 + CHUNKS].astype(f32)], axis=0)
    lane = lax.broadcasted_iota(jnp.int32, (16, 128), 1)
    wanted = (lane % 16 == ids[4] * 8 + ids[3] // 4) & (lane < 48)
    mixing = jnp.sum(jnp.where(wanted, told, 0.0), axis=1, keepdims=True)
    here = active(mine, 0, other, 256)
    there = active(other, 0, mine, 256)
    for k in range(14):
        lanes = slice(512 * k, 512 * k + 512)
        total = jnp.dot(here, down[:, lanes], preferred_element_type=f32)
        total = total + jnp.dot(there, down_other[:, lanes], preferred_element_type=f32)
        product[:, lanes] = total * mixing
    product[:, 7168:7296] = jnp.zeros((16, 128), f32)
    both = mine[0:8, 640:896] + other[0:8, 640:896]

    def fill(core):
        for k in range(32):
            at = (2 * k + core) * BLOCK
            base, turn = at // 128 * 128, at % 128
            for d in range(2):
                part = product[8 * d : 8 * d + 8, base : base + 256]
                if turn:
                    part = pltpu.roll(part, 256 - turn, 1)
                out[32 * d + k] = part[:, 0:128].astype(bf16)
        part = pltpu.roll(both, 256 - BLOCK, 1) if core else both
        own[...] = part[:, 0:128]

    @pl.when(ids[0] == 0)
    def _():
        fill(0)

    @pl.when(ids[0] == 1)
    def _():
        fill(1)


def finish_kernel(got, own, out):
    total = own[...]
    for i in range(64):
        total = total + got[i].astype(f32)
    for s in range(2):
        out[s] = total[4 * s : 4 * s + 4, 0:BLOCK].astype(bf16)


def body(
    prompt_pool,
    block_table,
    cache_len,
    queries,
    fresh_latent,
    x_in,
    routes,
    gates,
    norm_gain,
    value_up,
    out_proj,
    w_gate,
    w_up,
    w_down,
):
    gate_other, up_other, down_other = [
        swap(one, "core") for one in (w_gate[0], w_up[0], w_down[0])
    ]
    given = (
        queries.reshape(8, 64, 576),
        fresh_latent.reshape(2, 4, 576),
        x_in.reshape(2, 4, BLOCK),
        routes.reshape(2, 4, 8),
        gates.reshape(2, 4, 8),
        cache_len.reshape(1, 4),
        block_table[:, 0, 0],
    )
    picked, keys = call(
        pick_kernel,
        [shape(17, 16, 576), shape(16, 64, 576)],
        [FAR] * 8,
        tuple(far(one) for one in given + (prompt_pool[0, 0, 0],)),
        19000000,
        900000,
        [pltpu.VMEM(one.shape, one.dtype) for one in given[:6]]
        + [pltpu.SMEM((2, 4, 4), jnp.int32), pltpu.VMEM((5, 512, 128), f32)]
        + [pltpu.SemaphoreType.DMA((26,))],
        8,
    )
    q = swap(picked, "role")
    keys_other = swap(keys, "core")
    raising = pl.pallas_call(
        stash_kernel,
        out_shape=pltpu.VMEM((HALF, 512), bf16),
        in_specs=[FAR] * 4 + [ANY],
        out_specs=VM,
        scratch_shapes=[pltpu.SemaphoreType.DMA((4,))],
        compiler_params=pltpu.CompilerParams(vmem_limit_bytes=4 * MIB),
        cost_estimate=pl.CostEstimate(flops=0, bytes_accessed=7400000, transcendentals=0),
    )(
        *[far(one) for one in (w_gate[0], w_up[0], gate_other, up_other)],
        picked,
    )
    after = (raising, down_other)
    sent, told = call(
        attention_kernel,
        [shape(32, 8, 640), shape(16, 128, dtype=f32)],
        [VM, VM, VM] + [ANY] * len(after),
        (q, keys, keys_other) + after,
        300000000,
        4000000,
        [pltpu.VMEM((5, 256, 128), f32)],
        16,
        131072,
    )
    got = exchange(sent, XZ)
    vals, passed = call(
        context_kernel,
        [shape(8, 128), shape(CHUNKS, 8, 128)],
        [VM] * 4,
        (got, told, value_up[0], out_proj),
        12000000,
        1500000,
        (),
        8,
    )
    kept = call(
        kept_kernel,
        shape(CHUNKS, 8, 128, dtype=f32),
        [VM] * 3,
        (vals, told, out_proj),
        8000000,
        1000000,
        (),
        8,
    )
    partial = call(
        join_kernel, shape(32, 8, 128), [VM] * 2, (kept, swap(passed, "core")), 30000, 200000, (), 4
    )
    rows = exchange(
        call(
            spread_kernel,
            shape(64, 8, 128),
            [VM, VM],
            (exchange(partial, XZ), told),
            40000,
            200000,
            (),
            4,
        ),
        DXZ,
    )
    raised = call(
        raise_kernel,
        shape(16, 896, dtype=f32),
        [VM] * 3,
        (rows, norm_gain.reshape(56, 128), raising),
        60000000,
        6000000,
        [pltpu.VMEM((16, HALF), bf16), pltpu.VMEM((8, HALF), f32)],
        16,
    )
    raised_other = swap(raised, "core")
    outgoing, own = call(
        lower_kernel,
        [shape(64, 8, 128), shape(8, 128, dtype=f32)],
        [VM] * 5,
        (raised, raised_other, rows, w_down[0], down_other),
        60000000,
        4000000,
        [pltpu.VMEM((16, 7296), f32)],
        16,
        4096,
    )
    done = call(
        finish_kernel, shape(2, 4, BLOCK), [VM] * 2, (exchange(outgoing, DXZ), own), 70000, 140000, (), 4
    )
    return swap(done, "role").reshape(2, 1, 1, 4, BLOCK)


def solution(mesh):
    split = Mesh(mesh.devices.reshape(2, 2, 4, 8, 2), ("role", "dp", "x", "z", "core"))
    e = ("x", "z", "core")
    slab = ("dp", "x", "z", "core")
    placed = (
        P("role", "dp", e, None, None, None),
        P(None, "dp", e, None, None),
        P("role", "dp", None),
        P(None, "role", "dp", None, None, None),
        P(None, "role", "dp", None, None),
        P(None, "role", "dp", None, e),
        P(None, "role", "dp", None, None),
        P(None, "role", "dp", None, None),
        P(),
        P(e, None, None),
        P(e, None),
        P(slab, None, None),
        P(slab, None, None),
        P(slab, None, None),
    )
    return jax.shard_map(
        body,
        mesh=split,
        in_specs=placed,
        out_specs=P(None, "role", "dp", None, e),
        check_vma=False,
    )
```

```python
import jax
import jax.numpy as jnp
from jax import lax
from jax.experimental import pallas as pl
from jax.experimental.pallas import tpu as pltpu
from jax.sharding import Mesh, PartitionSpec as P

SCORE_SCALE = 192.0 ** (-0.5)
EPSILON = 1e-06
MASK_VALUE = -1e30
HALF = 3584
CHUNKS = 28
BLOCK = 112
XZ = ("x", "z")
DXZ = ("dp", "x", "z")
bf16 = jnp.bfloat16
f32 = jnp.float32

VM = pl.BlockSpec(memory_space=pltpu.VMEM)
ANY = pl.BlockSpec(memory_space=pl.ANY)
FAR = pl.BlockSpec(memory_space=pltpu.HBM)
MIB = 1024 * 1024


def call(kernel, outs, specs, args, flops, moved, scratch=(), limit=16, exps=0):
    many = isinstance(outs, list)
    return pl.pallas_call(
        kernel,
        out_shape=outs,
        in_specs=specs,
        out_specs=[VM] * len(outs) if many else VM,
        scratch_shapes=list(scratch),
        compiler_params=pltpu.CompilerParams(vmem_limit_bytes=limit * MIB),
        cost_estimate=pl.CostEstimate(flops=flops, bytes_accessed=moved, transcendentals=exps),
    )(*args)


def shape(*dims, dtype=bf16):
    return jax.ShapeDtypeStruct(dims, dtype)


def far(value):
    return pltpu.with_memory_space_constraint(value, pltpu.HBM)


def swap(value, axis):
    return lax.ppermute(value, axis, [(0, 1), (1, 0)])


def exchange(value, axes):
    return lax.all_to_all(value, axes, 0, 0, tiled=True)


def spot():
    core = lax.axis_index("core")
    chip = lax.axis_index("x") * 8 + lax.axis_index("z")
    return core, 1 - lax.axis_index("role"), chip * 2 + core, chip, lax.axis_index("dp")


def split(value):
    first = value.astype(bf16).astype(f32)
    second = (value - first).astype(bf16).astype(f32)
    return first, second, (value - first) - second


def pick_kernel(*refs):
    ids = spot()
    sources, pool, (out, keys), landed, (wide, sems) = refs[:7], refs[7], refs[8:10], refs[10:17], refs[17:]
    copies = [
        pltpu.make_async_copy(
            sources[0].at[pl.ds(2 * i, 2)], landed[0].at[pl.ds(2 * i, 2)], sems.at[i]
        )
        for i in range(4)
    ] + [pltpu.make_async_copy(sources[i], landed[i], sems.at[3 + i]) for i in range(1, 7)]
    copies[9].start()
    for one in copies[:9]:
        one.start()
    queries, fresh, x_in, routes, gates, lengths, table = landed
    copies[9].wait()
    gathered = [
        pltpu.make_async_copy(
            pool.at[table[ids[1], i // 4, i % 4]], keys.at[i], sems.at[10 + i]
        )
        for i in range(16)
    ]
    for one in gathered:
        one.start()
    for i in range(8):
        if i % 2 == 0:
            copies[i // 2].wait()
        asked = queries[i].astype(f32)
        for k in range(5):
            lanes = slice(128 * k, min(128 * k + 128, 576))
            wide[k, 64 * i : 64 * i + 64, 0 : lanes.stop - lanes.start] = asked[:, lanes]
        for k in range(5):
            lanes = slice(128 * k, min(128 * k + 128, 576))
            half = wide[k, pl.ds(64 * i + ids[0], 32, stride=2), :]
            half = half[:, 0 : lanes.stop - lanes.start].astype(bf16)
            out[2 * i, :, lanes] = half[0:16]
            out[2 * i + 1, :, lanes] = half[16:32]
    lane = lax.broadcasted_iota(jnp.int32, (4, 128), 1)
    for one in copies[4:9]:
        one.wait()
    count = jnp.concatenate([lengths[...], jnp.zeros((1, 124), jnp.int32)], axis=1)
    high = lax.shift_right_logical(count, 7)
    told = pltpu.roll(high.astype(f32), 64, 1) + pltpu.roll((count - 128 * high).astype(f32), 68, 1)
    rows = []
    blocks = []
    for s in range(2):
        note = jnp.zeros((4, 128), f32)
        for k in range(8):
            note = note + jnp.where(lane == routes[s][:, k : k + 1], gates[s][:, k : k + 1], 0.0)
        parts = split(note)
        note = parts[0] + pltpu.roll(parts[1], 16, 1) + pltpu.roll(parts[2], 32, 1) + told
        rows.append(fresh[s].astype(f32))
        block = jnp.concatenate([x_in[s].astype(f32), jnp.zeros((4, 16), f32)], axis=1)
        blocks.append(jnp.concatenate([block, note, jnp.zeros((4, 320), f32)], axis=1))
    out[16] = jnp.concatenate(rows + blocks, axis=0).astype(bf16)
    for one in gathered:
        one.wait()


def stash_kernel(*refs):
    ids = spot()
    sources, (raising, sems) = refs[:4], refs[5:]
    here = pl.ds(pl.multiple_of(ids[0] * HALF, 128), HALF)
    copies = [
        pltpu.make_async_copy(
            sources[i].at[here], raising.at[:, pl.ds(128 * i, 128)], sems.at[i]
        )
        for i in range(4)
    ]
    for one in copies:
        one.start()
    for one in copies:
        one.wait()


def attention_kernel(q, keys_mine, keys_other, *rest):
    ids = spot()
    out, told, scratch = rest[-3:]
    lane = lax.broadcasted_iota(jnp.int32, (1, 512), 1)
    start = jnp.where(lane < 256, ids[2] * 256, (ids[2] - 2 * ids[0]) * 256)
    places = (start + lane).astype(f32)
    slot = lax.broadcasted_iota(jnp.int32, (32, 128), 1)
    fresh = q[16]
    notes = fresh[:, 0:256].astype(f32)
    told[0:8, :] = notes[8:16, 0:128]
    told[8:16, :] = notes[8:16, 128:256]
    notes = notes[8:9, 128:256]
    row = lax.broadcasted_iota(jnp.int32, (64, 16), 0)
    col = lax.broadcasted_iota(jnp.int32, (64, 16), 1)
    keys, scores, late, weights, late_weights, top, total = ([None] * 4 for _ in range(7))
    for r in range(4):
        keys[r] = jnp.concatenate(
            [side[4 * r + j] for side in (keys_mine, keys_other) for j in range(4)], axis=0
        )
        asked = jnp.concatenate([q[2 * r], q[2 * r + 1], q[2 * r + 8], q[2 * r + 9]], axis=0)
        scores[r] = lax.dot_general(
            asked, keys[r], (((1,), (1,)), ((), ())), preferred_element_type=f32
        )
        late[r] = lax.dot_general(
            asked, fresh, (((1,), (1,)), ((), ())), preferred_element_type=f32
        )
    for r in range(4):
        usable = places < notes[0:1, 64 + r : 65 + r] * 128.0 + notes[0:1, 68 + r : 69 + r]
        counted = (ids[3] == 0) & ((col == r) | ((col == 4 + r) & (row >= 32)))
        scaled = jnp.where(usable, scores[r] * SCORE_SCALE, MASK_VALUE)
        late_scaled = jnp.where(counted, late[r] * SCORE_SCALE, MASK_VALUE)
        top[r] = jnp.maximum(
            jnp.max(scaled, axis=1, keepdims=True), jnp.max(late_scaled, axis=1, keepdims=True)
        )
        weights[r] = jnp.where(usable, jnp.exp(scaled - top[r]), 0.0)
        late_weights[r] = jnp.where(counted, jnp.exp(late_scaled - top[r]), 0.0)
        total[r] = jnp.sum(weights[r], axis=1, keepdims=True)
        total[r] = total[r] + jnp.sum(late_weights[r], axis=1, keepdims=True)
    for r in range(4):
        summed = jnp.dot(weights[r].astype(bf16), keys[r][:, :512], preferred_element_type=f32)
        summed = summed + jnp.dot(
            late_weights[r].astype(bf16), fresh[:, :512], preferred_element_type=f32
        )
        live = total[r] > 0.0
        safe = jnp.where(live, total[r], 1.0)
        level = jnp.where(live, top[r] + jnp.log(safe), MASK_VALUE)
        value = summed * (1.0 / safe)
        first, second, third = split(level)
        for s in range(2):
            rows = slice(32 * s, 32 * s + 32)
            tail = jnp.where(
                slot == 0,
                first[rows],
                jnp.where(slot == 1, second[rows], jnp.where(slot == 2, third[rows], 0.0)),
            )
            for k in range(5):
                part = value[rows, 128 * k : 128 * k + 128] if k < 4 else tail
                scratch[k, pl.ds(4 * s + r, 32, stride=8), :] = part
    for k in range(5):
        out[:, :, 128 * k : 128 * k + 128] = scratch[k].reshape(32, 8, 128).astype(bf16)


def project(ids, half, vals, told, proj, out):
    lanes = pl.ds(pl.multiple_of(half * HALF, 128), HALF)
    total = jnp.dot(vals[...], proj[:, lanes], preferred_element_type=f32)
    start = jnp.concatenate([told[0:8, :], jnp.zeros((8, HALF - 128), f32)], axis=1)
    start = pltpu.roll(start, (ids[2] % 32) * BLOCK, 1)
    total = total + jnp.where(ids[2] // 32 == half, start, 0.0)
    for k in range(CHUNKS):
        out[k] = total[:, 128 * k : 128 * k + 128].astype(out.dtype)
    for k in range(CHUNKS, 32):
        out[k] = jnp.zeros((8, 128), out.dtype)


def context_kernel(got, told, value_up, proj, vals, sent):
    ids = spot()
    level = jnp.sum(got[:, :, 512:640].astype(f32), axis=2, keepdims=True)
    factors = jnp.exp(level - jnp.max(level, axis=0, keepdims=True))
    denominator = jnp.sum(factors, axis=0)
    numerator = jnp.zeros((8, 512), f32)
    for i in range(32):
        numerator = numerator + factors[i] * got[i, :, 0:512].astype(f32)
    context = (numerator / denominator).astype(bf16)
    vals[...] = jnp.dot(context, value_up[...], preferred_element_type=f32).astype(bf16)
    project(ids, 1 - ids[0], vals, told, proj, sent)


def kept_kernel(vals, told, proj, kept):
    ids = spot()
    project(ids, ids[0], vals, told, proj, kept)


def join_kernel(kept, other, own, *outs):
    for k in range(4):
        group = pl.ds(lax.rem(lax.axis_index("x") + k, 4) * 8, 8)
        total = kept[group] + other[group].astype(f32)
        if k == 0:
            own[...] = total
        else:
            outs[k - 1][...] = total.astype(bf16)


def sum_kernel(own, first, second, third, out):
    total = own[...] + first[...].astype(f32) + second[...].astype(f32) + third[...].astype(f32)
    total = total.astype(bf16)
    for i in range(8):
        out[i] = total


def spread_kernel(got, told, out):
    for k in range(8):
        total = got[0, k].astype(f32)
        for i in range(1, 8):
            total = total + got[i, k].astype(f32)
        if k == CHUNKS % 8:
            total = jnp.where(lax.axis_index("x") == CHUNKS // 8, told[8:16, :], total)
        piece = total.astype(bf16)
        for i in range(8):
            out[i, k] = piece


def raise_kernel(rows, gain, weights, out, scaled, own):
    ids = spot()
    squares = [jnp.zeros((8, 128), f32) for _ in range(2)]
    for k in range(CHUNKS):
        lanes = slice(128 * k, 128 * k + 128)
        parts = [rows[32 * d + k].astype(f32) for d in range(2)]
        squares = [squares[d] + parts[d] * parts[d] for d in range(2)]
        both = jnp.concatenate(parts, axis=0) * gain[pl.ds(ids[0] * CHUNKS + k, 1), :]
        scaled[:, lanes] = both.astype(bf16)
        own[:, lanes] = jnp.where(ids[4] == 0, parts[0], parts[1])
    out[:, 0:512] = jnp.dot(scaled[...], weights[...], preferred_element_type=f32)
    out[:, 512:640] = jnp.concatenate(squares, axis=0)
    shift = HALF - (ids[3] % 16) * (2 * BLOCK)
    turned = pltpu.roll(own[...], shift, 1)[:, 0:256]
    out[0:8, 640:896] = jnp.where(ids[0] == ids[3] // 16, turned, 0.0)
    out[8:16, 640:896] = jnp.zeros((8, 256), f32)


def lower_kernel(mine, other, rows, down, down_other, out, own, product):
    ids = spot()
    squares = jnp.sum(mine[:, 512:640] + other[:, 512:640], axis=1, keepdims=True)
    scale = lax.rsqrt(squares * (1.0 / (2 * HALF)) + EPSILON)

    def active(near, near_at, far, far_at):
        gate = (near[:, near_at : near_at + 128] + far[:, far_at : far_at + 128]) * scale
        up = (
            near[:, near_at + 128 : near_at + 256] + far[:, far_at + 128 : far_at + 256]
        ) * scale
        return (gate / (1.0 + jnp.exp(-gate)) * up).astype(bf16)

    told = jnp.concatenate([rows[CHUNKS].astype(f32), rows[32 + CHUNKS].astype(f32)], axis=0)
    lane = lax.broadcasted_iota(jnp.int32, (16, 128), 1)
    wanted = (lane % 16 == ids[4] * 8 + ids[3] // 4) & (lane < 48)
    mixing = jnp.sum(jnp.where(wanted, told, 0.0), axis=1, keepdims=True)
    here = active(mine, 0, other, 256)
    there = active(other, 0, mine, 256)
    for k in range(14):
        lanes = slice(512 * k, 512 * k + 512)
        total = jnp.dot(here, down[:, lanes], preferred_element_type=f32)
        total = total + jnp.dot(there, down_other[:, lanes], preferred_element_type=f32)
        product[:, lanes] = total * mixing
    product[:, 7168:7296] = jnp.zeros((16, 128), f32)
    both = mine[0:8, 640:896] + other[0:8, 640:896]

    def fill(core):
        for k in range(32):
            at = (2 * k + core) * BLOCK
            base, turn = at // 128 * 128, at % 128
            for d in range(2):
                part = product[8 * d : 8 * d + 8, base : base + 256]
                if turn:
                    part = pltpu.roll(part, 256 - turn, 1)
                out[32 * d + k] = part[:, 0:128].astype(bf16)
        part = pltpu.roll(both, 256 - BLOCK, 1) if core else both
        own[...] = part[:, 0:128]

    @pl.when(ids[0] == 0)
    def _():
        fill(0)

    @pl.when(ids[0] == 1)
    def _():
        fill(1)


def finish_kernel(got, own, out):
    total = own[...]
    for i in range(64):
        total = total + got[i].astype(f32)
    for s in range(2):
        out[s] = total[4 * s : 4 * s + 4, 0:BLOCK].astype(bf16)


def body(
    prompt_pool,
    block_table,
    cache_len,
    queries,
    fresh_latent,
    x_in,
    routes,
    gates,
    norm_gain,
    value_up,
    out_proj,
    w_gate,
    w_up,
    w_down,
):
    gate_other, up_other, down_other = [
        swap(one, "core") for one in (w_gate[0], w_up[0], w_down[0])
    ]
    given = (
        queries.reshape(8, 64, 576),
        fresh_latent.reshape(2, 4, 576),
        x_in.reshape(2, 4, BLOCK),
        routes.reshape(2, 4, 8),
        gates.reshape(2, 4, 8),
        cache_len.reshape(1, 4),
        block_table[:, 0, 0],
    )
    picked, keys = call(
        pick_kernel,
        [shape(17, 16, 576), shape(16, 64, 576)],
        [FAR] * 8,
        tuple(far(one) for one in given + (prompt_pool[0, 0, 0],)),
        19000000,
        900000,
        [pltpu.VMEM(one.shape, one.dtype) for one in given[:6]]
        + [pltpu.SMEM((2, 4, 4), jnp.int32), pltpu.VMEM((5, 512, 128), f32)]
        + [pltpu.SemaphoreType.DMA((26,))],
        8,
    )
    q = swap(picked, "role")
    keys_other = swap(keys, "core")
    raising = pl.pallas_call(
        stash_kernel,
        out_shape=pltpu.VMEM((HALF, 512), bf16),
        in_specs=[FAR] * 4 + [ANY],
        out_specs=VM,
        scratch_shapes=[pltpu.SemaphoreType.DMA((4,))],
        compiler_params=pltpu.CompilerParams(vmem_limit_bytes=4 * MIB),
        cost_estimate=pl.CostEstimate(flops=0, bytes_accessed=7400000, transcendentals=0),
    )(
        *[far(one) for one in (w_gate[0], w_up[0], gate_other, up_other)],
        picked,
    )
    after = (raising, down_other)
    sent, told = call(
        attention_kernel,
        [shape(32, 8, 640), shape(16, 128, dtype=f32)],
        [VM, VM, VM] + [ANY] * len(after),
        (q, keys, keys_other) + after,
        300000000,
        4000000,
        [pltpu.VMEM((5, 256, 128), f32)],
        16,
        131072,
    )
    got = exchange(sent, XZ)
    vals, passed = call(
        context_kernel,
        [shape(8, 128), shape(32, 8, 128)],
        [VM] * 4,
        (got, told, value_up[0], out_proj),
        12000000,
        1500000,
        (),
        8,
    )
    kept = call(
        kept_kernel,
        shape(32, 8, 128, dtype=f32),
        [VM] * 3,
        (vals, told, out_proj),
        8000000,
        1000000,
        (),
        8,
    )
    own_x, *sent_x = call(
        join_kernel,
        [shape(8, 8, 128, dtype=f32)] + [shape(8, 8, 128)] * 3,
        [VM] * 2,
        (kept, swap(passed, "core")),
        30000,
        200000,
        (),
        4,
    )
    got_x = [
        lax.ppermute(one, "x", [(i, (i + k + 1) % 4) for i in range(4)])
        for k, one in enumerate(sent_x)
    ]
    sent_z = call(sum_kernel, shape(8, 8, 8, 128), [VM] * 4, (own_x, *got_x), 30000, 200000, (), 4)
    sent_rows = call(
        spread_kernel,
        shape(8, 8, 8, 128),
        [VM, VM],
        (exchange(sent_z, "z"), told),
        60000,
        260000,
        (),
        4,
    )
    rows = exchange(sent_rows, ("dp", "x")).reshape(64, 8, 128)
    raised = call(
        raise_kernel,
        shape(16, 896, dtype=f32),
        [VM] * 3,
        (rows, norm_gain.reshape(56, 128), raising),
        60000000,
        6000000,
        [pltpu.VMEM((16, HALF), bf16), pltpu.VMEM((8, HALF), f32)],
        16,
    )
    raised_other = swap(raised, "core")
    outgoing, own = call(
        lower_kernel,
        [shape(64, 8, 128), shape(8, 128, dtype=f32)],
        [VM] * 5,
        (raised, raised_other, rows, w_down[0], down_other),
        60000000,
        4000000,
        [pltpu.VMEM((16, 7296), f32)],
        16,
        4096,
    )
    done = call(
        finish_kernel, shape(2, 4, BLOCK), [VM] * 2, (exchange(outgoing, DXZ), own), 70000, 140000, (), 4
    )
    return swap(done, "role").reshape(2, 1, 1, 4, BLOCK)


def solution(mesh):
    split = Mesh(mesh.devices.reshape(2, 2, 4, 8, 2), ("role", "dp", "x", "z", "core"))
    e = ("x", "z", "core")
    slab = ("dp", "x", "z", "core")
    placed = (
        P("role", "dp", e, None, None, None),
        P(None, "dp", e, None, None),
        P("role", "dp", None),
        P(None, "role", "dp", None, None, None),
        P(None, "role", "dp", None, None),
        P(None, "role", "dp", None, e),
        P(None, "role", "dp", None, None),
        P(None, "role", "dp", None, None),
        P(),
        P(e, None, None),
        P(e, None),
        P(slab, None, None),
        P(slab, None, None),
        P(slab, None, None),
    )
    return jax.shard_map(
        body,
        mesh=split,
        in_specs=placed,
        out_specs=P(None, "role", "dp", None, e),
        check_vma=False,
    )
```
